512 devices in a mesh: row: 32 (over x, y, core), col: 16 (over z).
Axes of the slice: x: 4, y: 4, z: 16, core: 2. Of those that a mesh axis runs over, the one named last changes fastest.
Arguments:
- points: float32 [128, 65536], P(None, ('row', 'col')), may hold values from -6 to 6
- solution: float32 [16, 65536], P(None, ('row', 'col')), may hold values from -6 to 6
- residual: float32 [16, 65536], P(None, ('row', 'col')), may hold values from -23 to 23, as said below
- direction: float32 [16, 65536], P(None, ('row', 'col')), may hold values from -23 to 23, as said below
Outputs:
- next_solution: float32 [16, 65536], P(None, ('row', 'col'))
- next_residual: float32 [16, 65536], P(None, ('row', 'col'))
- next_direction: float32 [16, 65536], P(None, ('row', 'col'))
The draws below stay inside these ranges and needn't reach their ends.
Inputs may be any that keep to these rules, and one draw needn't show every extreme that they name: `residual`: Real-valued entries. `direction`: Real-valued entries.
All inputs are finite; a program needn't handle non-finite values.
Results may differ from the reference program's by a relative error of at most 0.00024.
Values sent between devices are 32-bit elements; how exact they have to be, the bound alone decides.
A program may use at most 64 MiB of HBM per device.

```python
import math
import jax
import jax.numpy as jnp
from jax import lax

WIDTH = 128
RHS = 16
POINTS = 65536


def apply_scales(seed_key, base_field):
    first_key, second_key = jax.random.split(seed_key, 2)
    position = jnp.arange(POINTS, dtype=jnp.float32) / POINTS
    point_part = jax.random.uniform(first_key, (1, POINTS), jnp.float32)
    side_part = jax.random.uniform(second_key, (RHS, 1), jnp.float32)
    log_scale = -0.75 + 0.5 * position[None, :] + 0.5 * point_part + 0.5 * side_part
    return base_field * jnp.exp(log_scale * math.log(10.0))


def draw_residual(seed_key, part_index):
    seed_key = jax.random.fold_in(seed_key, 11)
    scale_key, field_key = jax.random.split(seed_key, 2)
    base_field = jax.random.truncated_normal(field_key, -4.0, 4.0, (RHS, POINTS), jnp.float32)
    return apply_scales(scale_key, base_field)


def draw_direction(seed_key, part_index):
    seed_key = jax.random.fold_in(seed_key, 23)
    scale_key, field_key = jax.random.split(seed_key, 2)
    base_field = jax.random.truncated_normal(field_key, -4.0, 4.0, (RHS, POINTS), jnp.float32)
    return apply_scales(scale_key, base_field)


def levels(rng, dims, cuts, smallest, largest):
    gain, own = 1.0, jax.random.fold_in(rng, 6)
    for dim, shards_of in cuts:
        draws = jnp.exp(jax.random.uniform(jax.random.fold_in(own, dim), (shards_of,), jnp.float32, smallest / len(cuts), largest / len(cuts)))
        gain = gain * jnp.repeat(draws, dims[dim] // shards_of).reshape([-1 if axis == dim else 1 for axis in range(len(dims))])
    return gain


def gaussian(rng, dims, width, limit, cuts=(), kind=jnp.bfloat16):
    loudness = levels(rng, dims, cuts, -0.22, 0.18) if cuts else 1.0
    array = jax.random.normal(rng, dims, jnp.float32) * width * loudness
    return jnp.minimum(jnp.maximum(array, -limit), limit).astype(kind)


def setup_inputs(seed: int = 0) -> dict:
    arg_keys = jax.random.split(jax.random.key(seed), 5)
    return {
        "points": gaussian(arg_keys[0], (WIDTH, POINTS), 1.0, 6.0, ((1, 512),), jnp.float32),
        "solution": gaussian(arg_keys[1], (RHS, POINTS), 1.0, 6.0, ((1, 512),), jnp.float32),
        "residual": draw_residual(jax.random.fold_in(arg_keys[4], 71), 0),
        "direction": draw_direction(jax.random.fold_in(arg_keys[4], 71), 0),
    }


noise_var = 0.5
inv_two_len = 0.03125


def reference(points, solution, residual, direction):
    squares = jnp.sum(points * points, axis=0)
    block_rows = math.gcd(POINTS, 1024)

    def row_block(offset):
        rows_pts = lax.dynamic_slice_in_dim(points, offset, block_rows, 1)
        rows_sq = lax.dynamic_slice_in_dim(squares, offset, block_rows, 0)
        products = lax.dot_general(points, rows_pts, (((0,), (0,)), ((), ())), precision=lax.Precision.HIGHEST, preferred_element_type=jnp.float32)
        distance = squares[:, None] + rows_sq[None, :] - 2.0 * products
        kernel_tile = jnp.exp(-inv_two_len * distance)
        return jnp.dot(direction, kernel_tile, precision=lax.Precision.HIGHEST, preferred_element_type=jnp.float32)

    offsets = jnp.arange(POINTS // block_rows, dtype=jnp.int32) * block_rows
    stacked = lax.map(row_block, offsets)
    applied = jnp.transpose(stacked, (1, 0, 2)).reshape(RHS, POINTS) + noise_var * direction
    norm_now = jnp.sum(residual * residual, axis=1)
    curvature = jnp.sum(direction * applied, axis=1)
    step_size = norm_now / curvature
    next_solution = solution + step_size[:, None] * direction
    next_residual = residual - step_size[:, None] * applied
    norm_next = jnp.sum(next_residual * next_residual, axis=1)
    ratio = norm_next / norm_now
    next_direction = next_residual + ratio[:, None] * direction
    return (next_solution, next_residual, next_direction)
```

```python
import functools
import math

import jax
import jax.numpy as jnp
from jax import lax
from jax.experimental import pallas as pl
from jax.experimental.pallas import tpu as pltpu
from jax.sharding import PartitionSpec as P

noise_var = 0.5
inv_two_len = 0.03125
scale = inv_two_len * math.log2(math.e)

MESH = pl.DeviceIdType.MESH
f32 = jnp.float32
bf16 = jnp.bfloat16

side = 4
rows_n = 32
cols_n = 16
block = 128
rhs = 16
chunk = 1024
pairs = 8

offsets = sorted(
    [(dx, dy) for dx in range(side) for dy in range(side)],
    key=lambda d: (min(d[0], side - d[0]) + min(d[1], side - d[1]), max(min(d[0], side - d[0]), min(d[1], side - d[1]))),
)
plane = len(offsets)


def split(values):
    high = values.astype(bf16)
    low = (values - high.astype(f32)).astype(bf16)
    return high, low


def kernel(
    pts_ref,
    sol_ref,
    res_ref,
    dir_ref,
    nsol_ref,
    nres_ref,
    ndir_ref,
    col_in,
    row_in,
    weights,
    row_sq,
    stream,
    col_sq,
    dirs,
    tile_a,
    tile_b,
    total,
    part,
    part_in,
    stat_z,
    stat_r,
    col_send,
    col_recv,
    sib_send,
    sib_recv,
    row_send,
    row_recv,
    part_send,
    part_recv,
    sz_send,
    sz_recv,
    sr_send,
    sr_recv,
):
    r = lax.axis_index("row")
    z = lax.axis_index("col")
    x, y, core = r // 8, (r // 2) % 4, r % 2
    sibling = r + 1 - 2 * core
    up, down = (z + 1) % cols_n, (z + cols_n - 1) % cols_n

    barrier = pltpu.get_barrier_semaphore()

    @pl.loop(1, cols_n)
    def _(step):
        pl.semaphore_signal(barrier, inc=1, device_id=(r, (z + step) % cols_n), device_id_type=MESH)

    @pl.loop(1, rows_n)
    def _(step):
        pl.semaphore_signal(barrier, inc=1, device_id=((r + step) % rows_n, z), device_id_type=MESH)

    row_in[0] = pts_ref[...]
    col_in[0, 0, 0:block, :] = pts_ref[...].T
    col_in[0, 0, block : block + rhs, :] = dir_ref[...]
    total[...] = jnp.zeros_like(total)

    pl.semaphore_wait(barrier, cols_n - 1 + rows_n - 1)

    def row_copy(src, dst, target):
        return pltpu.make_async_remote_copy(
            src_ref=row_in.at[src],
            dst_ref=row_in.at[dst],
            send_sem=row_send.at[dst],
            recv_sem=row_recv.at[dst],
            device_id=(r, target),
            device_id_type=MESH,
        )

    def col_copy(o):
        dx, dy = offsets[o]
        target = (((x + side - dx) % side) * side + (y + side - dy) % side) * 2 + core
        return pltpu.make_async_remote_copy(
            src_ref=col_in.at[0, 0],
            dst_ref=col_in.at[0, o],
            send_sem=col_send.at[o],
            recv_sem=col_recv.at[o],
            device_id=(target, z),
            device_id_type=MESH,
        )

    def sib_copy(o):
        return pltpu.make_async_remote_copy(
            src_ref=col_in.at[0, o],
            dst_ref=col_in.at[1, o],
            send_sem=sib_send.at[o],
            recv_sem=sib_recv.at[o],
            device_id=(sibling, z),
            device_id_type=MESH,
        )

    def part_copy(slot, dst, target):
        return pltpu.make_async_remote_copy(
            src_ref=part.at[slot],
            dst_ref=part_in.at[dst],
            send_sem=part_send.at[slot],
            recv_sem=part_recv.at[dst],
            device_id=(r, target),
            device_id_type=MESH,
        )

    row_copy(0, 1, down).start()
    row_copy(0, 2, up).start()
    sib_copy(0).start()
    for o in range(1, plane):
        col_copy(o).start()

    def make_weights(p, half, slot):
        pts = row_in[slot]
        high, low = split(pts * (2.0 * scale))
        lanes = slice(half * block, (half + 1) * block)
        weights[p, 0 * block : 1 * block, lanes] = high
        weights[p, 1 * block : 2 * block, lanes] = low
        weights[p, 2 * block : 3 * block, lanes] = high
        weights[p, 3 * block : 4 * block, lanes] = low
        row_sq[p, :, lanes] = jnp.broadcast_to(scale * jnp.sum(pts * pts, axis=0, keepdims=True), (8, block))

    def make_stream(b, o):
        place = pl.ds(pl.multiple_of((2 * o + b) * block, block), block)
        pts = col_in[b, o, 0:block, :]
        high, low = split(pts)
        stream[place, 0 * block : 1 * block] = high
        stream[place, 1 * block : 2 * block] = high
        stream[place, 2 * block : 3 * block] = low
        stream[place, 3 * block : 4 * block] = low
        col_sq[place, :] = jnp.broadcast_to(scale * jnp.sum(pts * pts, axis=1, keepdims=True), (block, block))
        high, low = split(col_in[b, o, block : block + rhs, :])
        dirs[0:rhs, place] = high
        dirs[rhs : 2 * rhs, place] = low

    def take_columns(c):
        for i in range(4):
            o = 4 * c + i
            if o > 0:
                col_copy(o).wait_recv()
                sib_copy(o).start()
            make_stream(0, o)
        for i in range(4):
            o = 4 * c + i
            sib_copy(o).wait_recv()
            make_stream(1, o)

    def take_rows(p):
        first = 2 * p + 1
        row_copy(0, first, down).wait_recv()

        @pl.when(p < 7)
        def _():
            row_copy(first, first + 2, down).start()
            row_copy(0, first + 1, up).wait_recv()

            @pl.when(p < 6)
            def _():
                row_copy(first + 1, first + 3, up).start()

        make_weights(p, 0, first)
        make_weights(p, 1, (first + 1) % cols_n)

    def unit(u):
        m = jnp.where(u >= 9, 3, jnp.where(u >= 4, 2, jnp.where(u >= 1, 1, 0)))
        rest = u - m * m
        early = u < 16
        p = jnp.where(early, jnp.where(rest < m, rest, m), u // 4)
        c = jnp.where(early, jnp.where(rest < m, m, rest - m), u % 4)
        return p, c

    def prepare(u):
        for m in range(4):

            @pl.when(u == m * m)
            def _():
                take_rows(m)
                take_columns(m)

        @pl.when((u >= 16) & (u % 4 == 0) & (u < 32))
        def _():
            take_rows(u // 4)

    def products(u, tile):
        p, c = unit(u)
        place = pl.ds(pl.multiple_of(c * chunk, chunk), chunk)
        tile[...] = jnp.dot(stream[place, :], weights[p], preferred_element_type=f32)

    def apply(u, tile):
        p, c = unit(u)
        place = pl.ds(pl.multiple_of(c * chunk, chunk), chunk)
        sq = col_sq[place, :]
        exponent = tile[...] - jnp.concatenate([sq, sq], axis=1) - row_sq[p, 0:1, :]
        high, low = split(jnp.exp2(exponent))
        lhs = dirs[:, place]
        total[p] += jnp.dot(lhs, high, preferred_element_type=f32) + jnp.dot(lhs, low, preferred_element_type=f32)

    def finish(u):
        p, c = unit(u)

        @pl.when(c == 3)
        def _():
            both = total[p]
            both = both[0:rhs] + both[rhs : 2 * rhs]
            first = 2 * p + 1
            part[first] = both[:, 0:block]
            part[(first + 1) % cols_n] = both[:, block : 2 * block]

            @pl.when(p < 7)
            def _():
                part_copy(first, first + 1, (z + p + 1) % cols_n).start()
                part_copy(first + 1, first, (z + cols_n - p - 1) % cols_n).start()

            @pl.when(p == 7)
            def _():
                part_copy(15, 15, (z + 8) % cols_n).start()

    prepare(0)
    products(0, tile_a)

    @pl.loop(0, 16)
    def _(w):
        u = 2 * w
        prepare(u + 1)
        products(u + 1, tile_b)
        apply(u, tile_a)
        finish(u)
        prepare(u + 2)
        products(jnp.minimum(u + 2, 31), tile_a)
        apply(u + 1, tile_b)
        finish(u + 1)

    direction = dir_ref[...]
    residual = res_ref[...]
    applied = part[0] + noise_var * direction
    for slot in range(1, cols_n):
        part_copy(slot, slot, z).wait_recv()
        applied = applied + part_in[slot]

    lane = lax.broadcasted_iota(jnp.int32, (rhs, block), 1)
    line = lax.broadcasted_iota(jnp.int32, (rhs, block), 0)
    packed = jnp.zeros((rhs, block), f32)
    for q, values in enumerate((residual * residual, direction * applied, residual * applied, applied * applied)):
        packed = jnp.where(lane == line + q * rhs, jnp.sum(values, axis=1, keepdims=True), packed)
    stat_z[0] = jnp.sum(packed, axis=0, keepdims=True)

    def z_copy(step):
        return pltpu.make_async_remote_copy(
            src_ref=stat_z.at[0],
            dst_ref=stat_z.at[step],
            send_sem=sz_send.at[step],
            recv_sem=sz_recv.at[step],
            device_id=(r, (z + step) % cols_n),
            device_id_type=MESH,
        )

    def r_copy(step):
        return pltpu.make_async_remote_copy(
            src_ref=stat_r.at[0],
            dst_ref=stat_r.at[step],
            send_sem=sr_send.at[step],
            recv_sem=sr_recv.at[step],
            device_id=((r + step) % rows_n, z),
            device_id_type=MESH,
        )

    for step in range(1, cols_n):
        z_copy(step).start()
    for step in range(1, cols_n):
        z_copy(step).wait_recv()
    stat_r[0] = jnp.sum(stat_z[...], axis=0)
    for step in range(1, rows_n):
        r_copy(step).start()
    for step in range(1, rows_n):
        r_copy(step).wait_recv()
    sums = jnp.broadcast_to(jnp.sum(stat_r[...], axis=0), (rhs, block))

    def take(q):
        return jnp.sum(jnp.where(lane == line + q * rhs, sums, 0.0), axis=1, keepdims=True)

    norm_now, curvature, cross, square = take(0), take(1), take(2), take(3)
    step_size = norm_now / curvature
    norm_next = jnp.maximum(norm_now - step_size * (2.0 * cross - step_size * square), 0.0)
    ratio = norm_next / norm_now
    next_residual = residual - step_size * applied
    nsol_ref[...] = sol_ref[...] + step_size * direction
    nres_ref[...] = next_residual
    ndir_ref[...] = next_residual + ratio * direction

    for slot in range(1, cols_n):
        row_copy(0, slot, z).wait_send()
        part_copy(slot, slot, z).wait_send()
        z_copy(slot).wait_send()
    for o in range(plane):
        sib_copy(o).wait_send()
        if o > 0:
            col_copy(o).wait_send()
    for step in range(1, rows_n):
        r_copy(step).wait_send()


def per_device(points, solution, residual, direction):
    vmem = pl.BlockSpec(memory_space=pltpu.VMEM)
    dma = pltpu.SemaphoreType.DMA
    out = jax.ShapeDtypeStruct((rhs, block), f32)
    span = rows_n * block
    return pl.pallas_call(
        kernel,
        out_shape=(out, out, out),
        in_specs=[vmem] * 4,
        out_specs=(vmem, vmem, vmem),
        scratch_shapes=[
            pltpu.VMEM((2, plane, block + rhs, block), f32),
            pltpu.VMEM((cols_n, block, block), f32),
            pltpu.VMEM((pairs, 4 * block, 2 * block), bf16),
            pltpu.VMEM((pairs, 8, 2 * block), f32),
            pltpu.VMEM((span, 4 * block), bf16),
            pltpu.VMEM((span, block), f32),
            pltpu.VMEM((2 * rhs, span), bf16),
            pltpu.VMEM((chunk, 2 * block), f32),
            pltpu.VMEM((chunk, 2 * block), f32),
            pltpu.VMEM((pairs, 2 * rhs, 2 * block), f32),
            pltpu.VMEM((cols_n, rhs, block), f32),
            pltpu.VMEM((cols_n, rhs, block), f32),
            pltpu.VMEM((cols_n, 1, block), f32),
            pltpu.VMEM((rows_n, 1, block), f32),
            dma((plane,)),
            dma((plane,)),
            dma((plane,)),
            dma((plane,)),
            dma((cols_n,)),
            dma((cols_n,)),
            dma((cols_n,)),
            dma((cols_n,)),
            dma((cols_n,)),
            dma((cols_n,)),
            dma((rows_n,)),
            dma((rows_n,)),
        ],
        compiler_params=pltpu.CompilerParams(
            collective_id=0, has_side_effects=True, vmem_limit_bytes=48 * 1024 * 1024
        ),
        name="cg_step",
    )(points, solution, residual, direction)


def solution(mesh):
    spec = P(None, ("row", "col"))
    return jax.shard_map(
        per_device, mesh=mesh, in_specs=(spec,) * 4, out_specs=(spec,) * 3, check_vma=False
    )
```

```python
import functools
import math

import jax
import jax.numpy as jnp
from jax import lax
from jax.experimental import pallas as pl
from jax.experimental.pallas import tpu as pltpu
from jax.sharding import PartitionSpec as P

noise_var = 0.5
inv_two_len = 0.03125
scale = inv_two_len * math.log2(math.e)

MESH = pl.DeviceIdType.MESH
f32 = jnp.float32
bf16 = jnp.bfloat16

side = 4
rows_n = 32
cols_n = 16
block = 128
rhs = 16
chunk = 1024
pairs = 8

offsets = [
    (0, 0), (1, 0), (3, 0), (0, 1),
    (0, 3), (1, 1), (3, 3), (1, 3),
    (3, 1), (2, 0), (0, 2), (2, 1),
    (2, 3), (3, 2), (1, 2), (2, 2),
]
plane = len(offsets)
near = [(1, 0), (3, 0), (0, 1), (0, 3)]
diagonal = [(1, 1), (3, 3), (3, 1), (1, 3)]
relays = {
    (3, 0): [(3, 0)],
    (0, 3): [(0, 3)],
    (1, 1): [(1, 0), (1, 1)],
    (3, 3): [(3, 0)],
    (3, 1): [(0, 1)],
    (1, 3): [(0, 3)],
}
far = [o for o in offsets if o not in near + diagonal + [(0, 0)]]

units = [
    (0, 0), (1, 0), (2, 0), (2, 1), (1, 1), (0, 1), (3, 0), (3, 1),
    (4, 0), (4, 1), (2, 2), (3, 2), (4, 2), (2, 3), (3, 3), (4, 3),
    (5, 0), (5, 1), (5, 2), (5, 3), (6, 0), (6, 1), (6, 2), (6, 3),
    (7, 0), (7, 1), (7, 2), (7, 3), (1, 2), (1, 3), (0, 2), (0, 3),
]


def lookup(table, u):
    value = table[0]
    for i in range(1, len(table)):
        if table[i] != table[i - 1]:
            value = jnp.where(u >= i, table[i], value)
    return value


def split(values):
    high = values.astype(bf16)
    low = (values - high.astype(f32)).astype(bf16)
    return high, low


def kernel(
    pts_hbm,
    sol_hbm,
    res_hbm,
    dir_hbm,
    nsol_ref,
    nres_ref,
    ndir_ref,
    col_in,
    row_in,
    weights,
    row_sq,
    stream,
    col_sq,
    dirs,
    tile_a,
    tile_b,
    total,
    part,
    part_in,
    stat_z,
    stat_r,
    sol_ref,
    res_ref,
    dir_ref,
    load,
    col_send,
    col_recv,
    sib_send,
    sib_recv,
    row_send,
    row_recv,
    part_send,
    part_recv,
    sz_send,
    sz_recv,
    sr_send,
    sr_recv,
):
    r = lax.axis_index("row")
    z = lax.axis_index("col")
    x, y, core = r // 8, (r // 2) % 4, r % 2
    sibling = r + 1 - 2 * core
    up, down = (z + 1) % cols_n, (z + cols_n - 1) % cols_n

    loads = [
        pltpu.make_async_copy(src, dst, load.at[i])
        for i, (src, dst) in enumerate(
            ((pts_hbm, row_in.at[0]), (dir_hbm, dir_ref), (res_hbm, res_ref), (sol_hbm, sol_ref))
        )
    ]
    for copy in loads:
        copy.start()
    barrier = pltpu.get_barrier_semaphore()

    @pl.loop(1, cols_n)
    def _(step):
        pl.semaphore_signal(barrier, inc=1, device_id=(r, (z + step) % cols_n), device_id_type=MESH)

    @pl.loop(1, rows_n)
    def _(step):
        pl.semaphore_signal(barrier, inc=1, device_id=((r + step) % rows_n, z), device_id_type=MESH)

    for copy in loads:
        copy.wait()
    col_in[0, 0, 0:block, :] = row_in[0].T
    col_in[0, 0, block : block + rhs, :] = dir_ref[...]
    total[...] = jnp.zeros_like(total)

    pl.semaphore_wait(barrier, cols_n - 1 + rows_n - 1)

    def row_copy(src, dst, target):
        return pltpu.make_async_remote_copy(
            src_ref=row_in.at[src],
            dst_ref=row_in.at[dst],
            send_sem=row_send.at[dst],
            recv_sem=row_recv.at[dst],
            device_id=(r, target),
            device_id_type=MESH,
        )

    def slot_of(offset):
        return offsets.index((offset[0] % side, offset[1] % side))

    def col_copy(offset, step):
        target = (((x + side - step[0]) % side) * side + (y + side - step[1]) % side) * 2 + core
        dst = slot_of((offset[0] + step[0], offset[1] + step[1]))
        return pltpu.make_async_remote_copy(
            src_ref=col_in.at[0, slot_of(offset)],
            dst_ref=col_in.at[0, dst],
            send_sem=col_send.at[dst],
            recv_sem=col_recv.at[dst],
            device_id=(target, z),
            device_id_type=MESH,
        )

    def sib_copy(o):
        return pltpu.make_async_remote_copy(
            src_ref=col_in.at[0, o],
            dst_ref=col_in.at[1, o],
            send_sem=sib_send.at[o],
            recv_sem=sib_recv.at[o],
            device_id=(sibling, z),
            device_id_type=MESH,
        )

    def part_copy(slot, dst, target):
        return pltpu.make_async_remote_copy(
            src_ref=part.at[slot],
            dst_ref=part_in.at[dst],
            send_sem=part_send.at[slot],
            recv_sem=part_recv.at[dst],
            device_id=(r, target),
            device_id_type=MESH,
        )

    row_copy(0, 1, down).start()
    row_copy(0, 2, up).start()
    sib_copy(0).start()
    for offset in near + diagonal:
        col_copy((0, 0), offset).start()

    def make_weights(p, half, slot):
        pts = row_in[slot]
        high, low = split(pts * (2.0 * scale))
        lanes = slice(half * block, (half + 1) * block)
        weights[p, 0 * block : 1 * block, lanes] = high
        weights[p, 1 * block : 2 * block, lanes] = low
        weights[p, 2 * block : 3 * block, lanes] = high
        weights[p, 3 * block : 4 * block, lanes] = low
        row_sq[p, :, lanes] = jnp.broadcast_to(scale * jnp.sum(pts * pts, axis=0, keepdims=True), (8, block))

    def make_stream(b, o):
        place = pl.ds(pl.multiple_of((2 * o + b) * block, block), block)
        pts = col_in[b, o, 0:block, :]
        high, low = split(pts)
        stream[place, 0 * block : 1 * block] = high
        stream[place, 1 * block : 2 * block] = high
        stream[place, 2 * block : 3 * block] = low
        stream[place, 3 * block : 4 * block] = low
        col_sq[place, :] = jnp.broadcast_to(scale * jnp.sum(pts * pts, axis=1, keepdims=True), (block, block))
        high, low = split(col_in[b, o, block : block + rhs, :])
        dirs[0:rhs, place] = high
        dirs[rhs : 2 * rhs, place] = low

    def take_columns(arrived):
        for offset in arrived:
            col_copy((0, 0), offset).wait_recv()
            for step in relays.get(offset, ()):
                col_copy(offset, step).start()
            sib_copy(slot_of(offset)).start()

    def use_columns(c):
        for i in range(4):
            make_stream(0, 4 * c + i)
        for i in range(4):
            sib_copy(4 * c + i).wait_recv()
            make_stream(1, 4 * c + i)

    onward = {1: (1, 2), 2: (2,), 3: (2,), 4: (2,), 6: (1, 2)}

    def take_rows(d):
        plus, minus = 2 * d - 1, 2 * d
        row_copy(0, plus, z).wait_recv()
        for step in onward.get(d, ()):
            row_copy(plus, plus + 2 * step, (z + cols_n - step) % cols_n).start()
        if d < 8:
            row_copy(0, minus, z).wait_recv()
            for step in onward.get(d, ()):
                if d + step < 8:
                    row_copy(minus, minus + 2 * step, (z + step) % cols_n).start()
        make_weights(d - 1, 0, plus)
        make_weights(d - 1, 1, minus % cols_n)

    def event_0():
        take_rows(1)
        take_columns(near)
        use_columns(0)

    def event_1():
        take_rows(2)

    def event_2():
        take_columns(diagonal)
        take_rows(3)
        use_columns(1)

    def event_6():
        take_rows(4)

    def event_8():
        take_rows(5)
        take_columns(far)

    def event_10():
        use_columns(2)

    def event_13():
        use_columns(3)

    events = {
        1: event_1,
        2: event_2,
        6: event_6,
        8: event_8,
        10: event_10,
        13: event_13,
        16: lambda: take_rows(6),
        20: lambda: take_rows(7),
        24: lambda: take_rows(8),
    }

    def unit(u):
        return lookup([p for p, _ in units], u), lookup([c for _, c in units], u)

    def prepare(u, parity):
        for when, event in events.items():
            if when % 2 == parity:
                pl.when(u == when)(event)

    def products(u, tile):
        p, c = unit(u)
        place = pl.ds(pl.multiple_of(c * chunk, chunk), chunk)
        tile[...] = jnp.dot(stream[place, :], weights[p], preferred_element_type=f32)

    def apply(u, tile):
        p, c = unit(u)
        place = pl.ds(pl.multiple_of(c * chunk, chunk), chunk)
        sq = col_sq[place, :]
        exponent = tile[...] - jnp.concatenate([sq, sq], axis=1) - row_sq[p, 0:1, :]
        high, low = split(jnp.exp2(exponent))
        lhs = dirs[:, place]
        total[p] += jnp.dot(lhs, high, preferred_element_type=f32) + jnp.dot(lhs, low, preferred_element_type=f32)

    def finish(u):
        p, c = unit(u)

        @pl.when(c == 3)
        def _():
            both = total[p]
            both = both[0:rhs] + both[rhs : 2 * rhs]
            first = 2 * p + 1
            part[first] = both[:, 0:block]
            part[(first + 1) % cols_n] = both[:, block : 2 * block]

            @pl.when(p < 7)
            def _():
                part_copy(first, first + 1, (z + p + 1) % cols_n).start()
                part_copy(first + 1, first, (z + cols_n - p - 1) % cols_n).start()

            @pl.when(p == 7)
            def _():
                part_copy(15, 15, (z + 8) % cols_n).start()

    event_0()
    products(0, tile_a)

    @pl.loop(0, 16)
    def _(w):
        u = 2 * w
        prepare(u + 1, 1)
        products(u + 1, tile_b)
        apply(u, tile_a)
        finish(u)
        prepare(u + 2, 0)
        products(jnp.minimum(u + 2, 31), tile_a)
        apply(u + 1, tile_b)
        finish(u + 1)

    direction = dir_ref[...]
    residual = res_ref[...]
    applied = part[0] + noise_var * direction
    for slot in range(1, cols_n):
        part_copy(slot, slot, z).wait_recv()
        applied = applied + part_in[slot]

    lane = lax.broadcasted_iota(jnp.int32, (rhs, block), 1)
    line = lax.broadcasted_iota(jnp.int32, (rhs, block), 0)
    packed = jnp.zeros((rhs, block), f32)
    for q, values in enumerate((residual * residual, direction * applied, residual * applied, applied * applied)):
        packed = jnp.where(lane == line + q * rhs, jnp.sum(values, axis=1, keepdims=True), packed)
    stat_z[0] = jnp.sum(packed, axis=0, keepdims=True)

    def z_copy(step):
        return pltpu.make_async_remote_copy(
            src_ref=stat_z.at[0],
            dst_ref=stat_z.at[step],
            send_sem=sz_send.at[step],
            recv_sem=sz_recv.at[step],
            device_id=(r, (z + step) % cols_n),
            device_id_type=MESH,
        )

    def r_copy(step):
        return pltpu.make_async_remote_copy(
            src_ref=stat_r.at[0],
            dst_ref=stat_r.at[step],
            send_sem=sr_send.at[step],
            recv_sem=sr_recv.at[step],
            device_id=((r + step) % rows_n, z),
            device_id_type=MESH,
        )

    for step in range(1, cols_n):
        z_copy(step).start()
    for step in range(1, cols_n):
        z_copy(step).wait_recv()
    stat_r[0] = jnp.sum(stat_z[...], axis=0)
    for step in range(1, rows_n):
        r_copy(step).start()
    for step in range(1, rows_n):
        r_copy(step).wait_recv()
    sums = jnp.broadcast_to(jnp.sum(stat_r[...], axis=0), (rhs, block))

    def take(q):
        return jnp.sum(jnp.where(lane == line + q * rhs, sums, 0.0), axis=1, keepdims=True)

    norm_now, curvature, cross, square = take(0), take(1), take(2), take(3)
    step_size = norm_now / curvature
    norm_next = jnp.maximum(norm_now - step_size * (2.0 * cross - step_size * square), 0.0)
    ratio = norm_next / norm_now
    next_residual = residual - step_size * applied
    nsol_ref[...] = sol_ref[...] + step_size * direction
    nres_ref[...] = next_residual
    ndir_ref[...] = next_residual + ratio * direction

    for slot in range(1, cols_n):
        row_copy(0, slot, z).wait_send()
        part_copy(slot, slot, z).wait_send()
        z_copy(slot).wait_send()
    for o in range(plane):
        sib_copy(o).wait_send()
        if o > 0:
            col_copy((0, 0), offsets[o]).wait_send()
    for step in range(1, rows_n):
        r_copy(step).wait_send()


def per_device(points, solution, residual, direction):
    vmem = pl.BlockSpec(memory_space=pltpu.VMEM)
    dma = pltpu.SemaphoreType.DMA
    out = jax.ShapeDtypeStruct((rhs, block), f32)
    span = rows_n * block
    return pl.pallas_call(
        kernel,
        out_shape=(out, out, out),
        in_specs=[pl.BlockSpec(memory_space=pl.ANY)] * 4,
        out_specs=(vmem, vmem, vmem),
        scratch_shapes=[
            pltpu.VMEM((2, plane, block + rhs, block), f32),
            pltpu.VMEM((cols_n, block, block), f32),
            pltpu.VMEM((pairs, 4 * block, 2 * block), bf16),
            pltpu.VMEM((pairs, 8, 2 * block), f32),
            pltpu.VMEM((span, 4 * block), bf16),
            pltpu.VMEM((span, block), f32),
            pltpu.VMEM((2 * rhs, span), bf16),
            pltpu.VMEM((chunk, 2 * block), f32),
            pltpu.VMEM((chunk, 2 * block), f32),
            pltpu.VMEM((pairs, 2 * rhs, 2 * block), f32),
            pltpu.VMEM((cols_n, rhs, block), f32),
            pltpu.VMEM((cols_n, rhs, block), f32),
            pltpu.VMEM((cols_n, 1, block), f32),
            pltpu.VMEM((rows_n, 1, block), f32),
            pltpu.VMEM((rhs, block), f32),
            pltpu.VMEM((rhs, block), f32),
            pltpu.VMEM((rhs, block), f32),
            dma((4,)),
            dma((plane,)),
            dma((plane,)),
            dma((plane,)),
            dma((plane,)),
            dma((cols_n,)),
            dma((cols_n,)),
            dma((cols_n,)),
            dma((cols_n,)),
            dma((cols_n,)),
            dma((cols_n,)),
            dma((rows_n,)),
            dma((rows_n,)),
        ],
        compiler_params=pltpu.CompilerParams(
            collective_id=0, has_side_effects=True, vmem_limit_bytes=48 * 1024 * 1024
        ),
        name="cg_step",
    )(points, solution, residual, direction)


def solution(mesh):
    spec = P(None, ("row", "col"))
    return jax.shard_map(
        per_device, mesh=mesh, in_specs=(spec,) * 4, out_specs=(spec,) * 3, check_vma=False
    )
```

```python
import math

import jax
import jax.numpy as jnp
from jax import lax
from jax.experimental import pallas as pl
from jax.experimental.pallas import tpu as pltpu
from jax.sharding import PartitionSpec as P

noise_var = 0.5
inv_two_len = 0.03125
scale = inv_two_len * math.log2(math.e)

MESH = pl.DeviceIdType.MESH
f32 = jnp.float32
bf16 = jnp.bfloat16

side = 4
rows_n = 32
cols_n = 16
block = 128
rhs = 16
chunk = 1024
chunks = 4
pairs = 4
held = 9

offsets = [
    (0, 0), (1, 0), (3, 0), (0, 1),
    (0, 3), (1, 1), (3, 3), (1, 3),
    (3, 1), (2, 0), (0, 2), (2, 1),
    (2, 3), (3, 2), (1, 2), (2, 2),
]
plane = len(offsets)
near = [(1, 0), (3, 0), (0, 1), (0, 3)]
diagonal = [(1, 1), (3, 3), (3, 1), (1, 3)]
far = [o for o in offsets if o not in near + diagonal + [(0, 0)]]
relays = {
    (3, 0): [(3, 0)],
    (0, 3): [(0, 3)],
    (1, 1): [(1, 0), (1, 1)],
    (3, 3): [(3, 0)],
    (3, 1): [(0, 1)],
    (1, 3): [(0, 3)],
}

units = [
    (0, 0), (1, 0), (0, 1), (1, 1), (2, 0), (2, 1), (3, 0), (3, 1),
    (3, 2), (2, 2), (1, 2), (0, 2), (3, 3), (2, 3), (1, 3), (0, 3),
]


def lookup(table, u):
    value = table[0]
    for i in range(1, len(table)):
        if table[i] != table[i - 1]:
            value = jnp.where(u >= i, table[i], value)
    return value


def slot_of(offset):
    return offsets.index((offset[0] % side, offset[1] % side))


def split(values):
    high = values.astype(bf16)
    low = (values - high.astype(f32)).astype(bf16)
    return high, low


def dot(a, b):
    return jnp.dot(a, b, preferred_element_type=f32)


def dot_turned(a, b):
    return lax.dot_general(a, b, (((1,), (1,)), ((), ())), preferred_element_type=f32)


def kernel(
    pts_hbm,
    sol_hbm,
    res_hbm,
    dir_hbm,
    nsol_ref,
    nres_ref,
    ndir_ref,
    col_in,
    row_in,
    weights,
    row_sq,
    row_dirs,
    stream,
    col_sq,
    dirs,
    own_weights,
    own_sq,
    tile_a,
    tile_b,
    own_a,
    own_b,
    row_total,
    col_total,
    own_total,
    part,
    part_in,
    col_part,
    col_part_in,
    stat_z,
    stat_r,
    sol_ref,
    res_ref,
    load,
    col_send,
    col_recv,
    sib_send,
    sib_recv,
    row_send,
    row_recv,
    part_send,
    part_recv,
    cp_send,
    cp_recv,
    sz_send,
    sz_recv,
    sr_send,
    sr_recv,
):
    r = lax.axis_index("row")
    z = lax.axis_index("col")
    x, y, core = r // 8, (r // 2) % 4, r % 2
    sibling = r + 1 - 2 * core

    loads = [
        pltpu.make_async_copy(src, dst, load.at[i])
        for i, (src, dst) in enumerate(
            (
                (pts_hbm, row_in.at[0, 0:block]),
                (dir_hbm, row_in.at[0, block : block + rhs]),
                (res_hbm, res_ref),
                (sol_hbm, sol_ref),
            )
        )
    ]
    for copy in loads:
        copy.start()

    barrier = pltpu.get_barrier_semaphore()
    for step in (4, 12, 3, 13, 2, 14, 1, 15):
        pl.semaphore_signal(barrier, inc=1, device_id=(r, (z + step) % cols_n), device_id_type=MESH)

    @pl.loop(1, rows_n)
    def _(step):
        pl.semaphore_signal(barrier, inc=1, device_id=((r + step) % rows_n, z), device_id_type=MESH)

    for copy in loads:
        copy.wait()
    col_in[0, 0, 0:block, :] = row_in[0, 0:block, :].T
    col_in[0, 0, block : block + rhs, :] = row_in[0, block : block + rhs, :]
    row_total[...] = jnp.zeros_like(row_total)
    col_total[...] = jnp.zeros_like(col_total)
    own_total[...] = jnp.zeros_like(own_total)

    pl.semaphore_wait(barrier, 8 + rows_n - 1)

    def row_copy(src, dst, step):
        return pltpu.make_async_remote_copy(
            src_ref=row_in.at[src],
            dst_ref=row_in.at[dst],
            send_sem=row_send.at[dst],
            recv_sem=row_recv.at[dst],
            device_id=(r, (z + cols_n + step) % cols_n),
            device_id_type=MESH,
        )

    def device_at(offset, other):
        target = (((x + offset[0]) % side) * side + (y + offset[1]) % side) * 2
        return target + (1 - core if other else core)

    def col_copy(offset, step):
        dst = slot_of((offset[0] + step[0], offset[1] + step[1]))
        return pltpu.make_async_remote_copy(
            src_ref=col_in.at[0, slot_of(offset)],
            dst_ref=col_in.at[0, dst],
            send_sem=col_send.at[dst],
            recv_sem=col_recv.at[dst],
            device_id=(device_at((side - step[0], side - step[1]), False), z),
            device_id_type=MESH,
        )

    def sib_copy(o):
        return pltpu.make_async_remote_copy(
            src_ref=col_in.at[0, o],
            dst_ref=col_in.at[1, o],
            send_sem=sib_send.at[o],
            recv_sem=sib_recv.at[o],
            device_id=(sibling, z),
            device_id_type=MESH,
        )

    def part_copy(k):
        return pltpu.make_async_remote_copy(
            src_ref=part.at[k],
            dst_ref=part_in.at[k],
            send_sem=part_send.at[k],
            recv_sem=part_recv.at[k],
            device_id=(r, (z + (cols_n - k if k % 2 else k)) % cols_n),
            device_id_type=MESH,
        )

    def col_part_copy(b, o):
        dx, dy = offsets[o]
        dst = slot_of((-dx, -dy))
        return pltpu.make_async_remote_copy(
            src_ref=col_part.at[b, o],
            dst_ref=col_part_in.at[b, dst],
            send_sem=cp_send.at[b, o],
            recv_sem=cp_recv.at[b, dst],
            device_id=(device_at((dx, dy), b == 1), z),
            device_id_type=MESH,
        )

    row_copy(0, 3, 3).start()
    row_copy(0, 4, -4).start()
    row_copy(0, 1, 1).start()
    row_copy(0, 2, -2).start()
    sib_copy(0).start()
    for offset in near + diagonal:
        col_copy((0, 0), offset).start()

    def turn(pts):
        high, low = split(pts * (2.0 * scale))
        stacked = jnp.concatenate([high, low, high, low], axis=0)
        return stacked, jnp.broadcast_to(scale * jnp.sum(pts * pts, axis=0, keepdims=True), (8, block))

    def make_weights(p):
        for half in range(2):
            k = 2 * p + 1 + half
            lanes = slice(half * block, (half + 1) * block)
            weights[p, :, lanes], row_sq[p, :, lanes] = turn(row_in[k, 0:block, :])
            if k < 8:
                high, low = split(row_in[k, block : block + rhs, :])
            else:
                high = low = jnp.zeros((rhs, block), bf16)
            row_dirs[p, 0:rhs, lanes] = high
            row_dirs[p, rhs : 2 * rhs, lanes] = low

    def make_stream(b, o):
        place = pl.ds(pl.multiple_of((2 * o + b) * block, block), block)
        pts = col_in[b, o, 0:block, :]
        high, low = split(pts)
        stream[place, 0 * block : 1 * block] = high
        stream[place, 1 * block : 2 * block] = high
        stream[place, 2 * block : 3 * block] = low
        stream[place, 3 * block : 4 * block] = low
        col_sq[place, :] = jnp.broadcast_to(scale * jnp.sum(pts * pts, axis=1, keepdims=True), (block, block))
        high, low = split(col_in[b, o, block : block + rhs, :])
        dirs[0:rhs, place] = high
        dirs[rhs : 2 * rhs, place] = low

    def take_columns(arrived):
        for offset in arrived:
            col_copy((0, 0), offset).wait_recv()
            for step in relays.get(offset, ()):
                col_copy(offset, step).start()
            sib_copy(slot_of(offset)).start()

    def use_columns(c):
        @pl.loop(4 * c, 4 * c + 4)
        def _(o):
            make_stream(0, o)

        @pl.loop(4 * c, 4 * c + 4)
        def _(o):
            sib_copy(o).wait_recv()
            make_stream(1, o)

    def take_row(k):
        row_copy(0, k, 0).wait_recv()
        if k == 3:
            row_copy(3, 5, 2).start()
            row_copy(3, 7, 4).start()
        if k == 4:
            row_copy(4, 6, -2).start()
            row_copy(4, 8, -4).start()

    def event_0():
        take_columns(near)
        take_row(1)
        take_row(2)
        make_weights(0)
        take_row(3)
        take_row(4)
        use_columns(0)

    def event_1():
        make_weights(1)

    def event_2():
        take_columns(diagonal)
        use_columns(1)

    def event_4():
        take_row(5)
        take_row(6)
        make_weights(2)

    def event_6():
        take_row(7)
        take_row(8)
        make_weights(3)

    def event_7():
        take_columns(far)

    def event_8():
        use_columns(2)

    def event_12():
        use_columns(3)

    events = {1: event_1, 2: event_2, 4: event_4, 6: event_6, 7: event_7, 8: event_8, 12: event_12}

    def send_rows(p):
        both = row_total[p]
        both = both[0:rhs] + both[rhs : 2 * rhs]
        for half in range(2):
            k = 2 * p + 1 + half
            part[k] = both[:, half * block : (half + 1) * block]
            part_copy(k).start()

    def send_columns(c):
        for o in range(4 * c, 4 * c + 4):
            for b in range(2):
                place = slice((2 * o + b) * block, (2 * o + b + 1) * block)
                col_part[b, o] = col_total[0:rhs, place] + col_total[rhs : 2 * rhs, place]
                if (b, o) != (0, 0):
                    col_part_copy(b, o).start()

    def finish_7():
        send_columns(0)
        send_columns(1)

    def finish_15():
        send_columns(3)
        send_rows(0)

    finishes = {
        7: finish_7,
        11: lambda: send_columns(2),
        12: lambda: send_rows(3),
        13: lambda: send_rows(2),
        14: lambda: send_rows(1),
        15: finish_15,
    }

    def unit(u):
        return lookup([p for p, _ in units], u), lookup([c for _, c in units], u)

    def run(table, u, parity):
        for when, event in table.items():
            if when % 2 == parity:
                pl.when(u == when)(event)

    def products(u, tile):
        p, c = unit(u)
        place = pl.ds(pl.multiple_of(c * chunk, chunk), chunk)
        tile[...] = dot(stream[place, :], weights[p])

    def apply(u, tile):
        p, c = unit(u)
        place = pl.ds(pl.multiple_of(c * chunk, chunk), chunk)
        sq = col_sq[place, :]
        exponent = tile[...] - jnp.concatenate([sq, sq], axis=1) - row_sq[p, 0:1, :]
        high, low = split(jnp.exp2(exponent))
        row_total[p] += dot(dirs[:, place], high) + dot(dirs[:, place], low)
        col_total[:, place] += dot_turned(row_dirs[p], high) + dot_turned(row_dirs[p], low)

    event_0()
    products(0, tile_a)

    @pl.loop(0, len(units) // 2)
    def _(w):
        u = 2 * w
        run(events, u + 1, 1)
        products(u + 1, tile_b)
        apply(u, tile_a)
        run(finishes, u, 0)
        run(events, u + 2, 0)
        products(jnp.minimum(u + 2, len(units) - 1), tile_a)
        apply(u + 1, tile_b)
        run(finishes, u + 1, 1)

    own_weights[...], own_sq[...] = turn(row_in[0, 0:block, :])

    def own_products(c, tile):
        place = pl.ds(pl.multiple_of(c * chunk, chunk), chunk)
        tile[...] = dot(stream[place, :], own_weights[...])

    def own_apply(c, tile):
        place = pl.ds(pl.multiple_of(c * chunk, chunk), chunk)
        high, low = split(jnp.exp2(tile[...] - col_sq[place, :] - own_sq[0:1, :]))
        own_total[...] += dot(dirs[:, place], high) + dot(dirs[:, place], low)

    own_products(0, own_a)

    @pl.loop(0, chunks // 2)
    def _(w):
        c = 2 * w
        own_products(c + 1, own_b)
        own_apply(c, own_a)
        own_products(jnp.minimum(c + 2, chunks - 1), own_a)
        own_apply(c + 1, own_b)

    direction = row_in[0, block : block + rhs, :]
    residual = res_ref[...]
    applied = own_total[0:rhs] + own_total[rhs : 2 * rhs] + col_part[0, 0] + noise_var * direction
    for k in range(8, 0, -1):
        part_copy(k).wait_recv()
        applied = applied + part_in[k]
    for o in range(plane):
        for b in range(2):
            if (b, o) != (0, 0):
                col_part_copy(b, o).wait_recv()
                applied = applied + col_part_in[b, slot_of((-offsets[o][0], -offsets[o][1]))]

    lane = lax.broadcasted_iota(jnp.int32, (rhs, block), 1)
    line = lax.broadcasted_iota(jnp.int32, (rhs, block), 0)
    packed = jnp.zeros((rhs, block), f32)
    for q, values in enumerate((residual * residual, direction * applied, residual * applied, applied * applied)):
        packed = jnp.where(lane == line + q * rhs, jnp.sum(values, axis=1, keepdims=True), packed)
    stat_z[0] = jnp.sum(packed, axis=0, keepdims=True)

    def z_copy(step):
        return pltpu.make_async_remote_copy(
            src_ref=stat_z.at[0],
            dst_ref=stat_z.at[step],
            send_sem=sz_send.at[step],
            recv_sem=sz_recv.at[step],
            device_id=(r, (z + step) % cols_n),
            device_id_type=MESH,
        )

    def r_copy(step):
        return pltpu.make_async_remote_copy(
            src_ref=stat_r.at[0],
            dst_ref=stat_r.at[step],
            send_sem=sr_send.at[step],
            recv_sem=sr_recv.at[step],
            device_id=((r + step) % rows_n, z),
            device_id_type=MESH,
        )

    for step in sorted(range(1, cols_n), key=lambda step: -min(step, cols_n - step)):
        z_copy(step).start()
    for step in range(1, cols_n):
        z_copy(step).wait_recv()
    stat_r[0] = jnp.sum(stat_z[...], axis=0)
    for step in range(1, rows_n):
        r_copy(step).start()
    for step in range(1, rows_n):
        r_copy(step).wait_recv()
    sums = jnp.broadcast_to(jnp.sum(stat_r[...], axis=0), (rhs, block))

    def take(q):
        return jnp.sum(jnp.where(lane == line + q * rhs, sums, 0.0), axis=1, keepdims=True)

    norm_now, curvature, cross, square = take(0), take(1), take(2), take(3)
    step_size = norm_now / curvature
    norm_next = jnp.maximum(norm_now - step_size * (2.0 * cross - step_size * square), 0.0)
    ratio = norm_next / norm_now
    next_residual = residual - step_size * applied
    nsol_ref[...] = sol_ref[...] + step_size * direction
    nres_ref[...] = next_residual
    ndir_ref[...] = next_residual + ratio * direction

    for k in range(1, held):
        row_copy(0, k, 0).wait_send()
        part_copy(k).wait_send()
    for step in range(1, cols_n):
        z_copy(step).wait_send()
    for step in range(1, rows_n):
        r_copy(step).wait_send()
    for o in range(plane):
        sib_copy(o).wait_send()
        if o > 0:
            col_copy((0, 0), offsets[o]).wait_send()
        for b in range(2):
            if (b, o) != (0, 0):
                col_part_copy(b, o).wait_send()


def per_device(points, solution, residual, direction):
    vmem = pl.BlockSpec(memory_space=pltpu.VMEM)
    dma = pltpu.SemaphoreType.DMA
    out = jax.ShapeDtypeStruct((rhs, block), f32)
    span = rows_n * block
    return pl.pallas_call(
        kernel,
        out_shape=(out, out, out),
        in_specs=[pl.BlockSpec(memory_space=pltpu.HBM)] * 4,
        out_specs=(vmem, vmem, vmem),
        scratch_shapes=[
            pltpu.VMEM((2, plane, block + rhs, block), f32),
            pltpu.VMEM((held, block + rhs, block), f32),
            pltpu.VMEM((pairs, 4 * block, 2 * block), bf16),
            pltpu.VMEM((pairs, 8, 2 * block), f32),
            pltpu.VMEM((pairs, 2 * rhs, 2 * block), bf16),
            pltpu.VMEM((span, 4 * block), bf16),
            pltpu.VMEM((span, block), f32),
            pltpu.VMEM((2 * rhs, span), bf16),
            pltpu.VMEM((4 * block, block), bf16),
            pltpu.VMEM((8, block), f32),
            pltpu.VMEM((chunk, 2 * block), f32),
            pltpu.VMEM((chunk, 2 * block), f32),
            pltpu.VMEM((chunk, block), f32),
            pltpu.VMEM((chunk, block), f32),
            pltpu.VMEM((pairs, 2 * rhs, 2 * block), f32),
            pltpu.VMEM((2 * rhs, span), f32),
            pltpu.VMEM((2 * rhs, block), f32),
            pltpu.VMEM((held, rhs, block), f32),
            pltpu.VMEM((held, rhs, block), f32),
            pltpu.VMEM((2, plane, rhs, block), f32),
            pltpu.VMEM((2, plane, rhs, block), f32),
            pltpu.VMEM((cols_n, 1, block), f32),
            pltpu.VMEM((rows_n, 1, block), f32),
            pltpu.VMEM((rhs, block), f32),
            pltpu.VMEM((rhs, block), f32),
            dma((4,)),
            dma((plane,)),
            dma((plane,)),
            dma((plane,)),
            dma((plane,)),
            dma((held,)),
            dma((held,)),
            dma((held,)),
            dma((held,)),
            dma((2, plane)),
            dma((2, plane)),
            dma((cols_n,)),
            dma((cols_n,)),
            dma((rows_n,)),
            dma((rows_n,)),
        ],
        compiler_params=pltpu.CompilerParams(
            collective_id=0, has_side_effects=True, vmem_limit_bytes=60 * 1024 * 1024
        ),
        name="cg_step",
    )(points, solution, residual, direction)


def solution(mesh):
    spec = P(None, ("row", "col"))
    return jax.shard_map(
        per_device, mesh=mesh, in_specs=(spec,) * 4, out_specs=(spec,) * 3, check_vma=False
    )
```

```python
import math

import jax
import jax.numpy as jnp
from jax import lax
from jax.experimental import pallas as pl
from jax.experimental.pallas import tpu as pltpu
from jax.sharding import PartitionSpec as P

noise_var = 0.5
inv_two_len = 0.03125
scale = inv_two_len * math.log2(math.e)

MESH = pl.DeviceIdType.MESH
f32 = jnp.float32
bf16 = jnp.bfloat16

side = 4
rows_n = 32
cols_n = 16
block = 128
rhs = 16
chunk = 1024
chunks = 4
pairs = 4
held = 9

offsets = [
    (0, 0), (1, 0), (3, 0), (0, 1),
    (0, 3), (1, 1), (3, 3), (1, 3),
    (3, 1), (2, 0), (0, 2), (2, 1),
    (2, 3), (3, 2), (1, 2), (2, 2),
]
plane = len(offsets)
near = [(1, 0), (3, 0), (0, 1), (0, 3)]
diagonal = [(1, 1), (3, 3), (3, 1), (1, 3)]
far = [o for o in offsets if o not in near + diagonal + [(0, 0)]]
relays = {
    (3, 0): [(3, 0)],
    (0, 3): [(0, 3)],
    (1, 1): [(1, 0), (1, 1)],
    (3, 3): [(3, 0)],
    (3, 1): [(0, 1)],
    (1, 3): [(0, 3)],
}

units = [
    (0, 0), (0, 1), (1, 0), (1, 1), (1, 2), (1, 3), (0, 2), (0, 3),
    (2, 0), (2, 1), (2, 2), (2, 3), (3, 0), (3, 1), (3, 2), (3, 3),
]


def lookup(table, u):
    value = table[0]
    for i in range(1, len(table)):
        if table[i] != table[i - 1]:
            value = jnp.where(u >= i, table[i], value)
    return value


def slot_of(offset):
    return offsets.index((offset[0] % side, offset[1] % side))


def split(values):
    high = values.astype(bf16)
    low = (values - high.astype(f32)).astype(bf16)
    return high, low


def dot(a, b):
    return jnp.dot(a, b, preferred_element_type=f32)


def dot_turned(a, b):
    return lax.dot_general(a, b, (((1,), (1,)), ((), ())), preferred_element_type=f32)


def kernel(
    pts_hbm,
    sol_hbm,
    res_hbm,
    dir_hbm,
    nsol_ref,
    nres_ref,
    ndir_ref,
    col_in,
    row_in,
    weights,
    row_sq,
    row_dirs,
    stream,
    col_sq,
    dirs,
    own_weights,
    own_sq,
    tile_a,
    tile_b,
    own_a,
    own_b,
    row_total,
    col_total,
    own_total,
    part,
    part_in,
    col_part,
    col_part_in,
    stat_z,
    stat_r,
    sol_ref,
    res_ref,
    load,
    col_send,
    col_recv,
    sib_send,
    sib_recv,
    row_send,
    row_recv,
    part_send,
    part_recv,
    cp_send,
    cp_recv,
    sz_send,
    sz_recv,
    sr_send,
    sr_recv,
):
    r = lax.axis_index("row")
    z = lax.axis_index("col")
    x, y, core = r // 8, (r // 2) % 4, r % 2
    sibling = r + 1 - 2 * core

    loads = [
        pltpu.make_async_copy(src, dst, load.at[i])
        for i, (src, dst) in enumerate(
            (
                (pts_hbm, row_in.at[0, 0:block]),
                (dir_hbm, row_in.at[0, block : block + rhs]),
                (res_hbm, res_ref),
                (sol_hbm, sol_ref),
            )
        )
    ]
    for copy in loads:
        copy.start()

    barrier = pltpu.get_barrier_semaphore()
    for step in (4, 12, 3, 13, 2, 14, 1, 15):
        pl.semaphore_signal(barrier, inc=1, device_id=(r, (z + step) % cols_n), device_id_type=MESH)

    @pl.loop(1, rows_n)
    def _(step):
        pl.semaphore_signal(barrier, inc=1, device_id=((r + step) % rows_n, z), device_id_type=MESH)

    for copy in loads:
        copy.wait()
    col_in[0, 0, 0:block, :] = row_in[0, 0:block, :].T
    col_in[0, 0, block : block + rhs, :] = row_in[0, block : block + rhs, :]
    row_total[...] = jnp.zeros_like(row_total)
    col_total[...] = jnp.zeros_like(col_total)
    own_total[...] = jnp.zeros_like(own_total)

    pl.semaphore_wait(barrier, 8 + rows_n - 1)

    def row_copy(src, dst, step):
        return pltpu.make_async_remote_copy(
            src_ref=row_in.at[src],
            dst_ref=row_in.at[dst],
            send_sem=row_send.at[dst],
            recv_sem=row_recv.at[dst],
            device_id=(r, (z + cols_n + step) % cols_n),
            device_id_type=MESH,
        )

    def device_at(offset, other):
        target = (((x + offset[0]) % side) * side + (y + offset[1]) % side) * 2
        return target + (1 - core if other else core)

    def col_copy(offset, step):
        dst = slot_of((offset[0] + step[0], offset[1] + step[1]))
        return pltpu.make_async_remote_copy(
            src_ref=col_in.at[0, slot_of(offset)],
            dst_ref=col_in.at[0, dst],
            send_sem=col_send.at[dst],
            recv_sem=col_recv.at[dst],
            device_id=(device_at((side - step[0], side - step[1]), False), z),
            device_id_type=MESH,
        )

    def sib_copy(o):
        return pltpu.make_async_remote_copy(
            src_ref=col_in.at[0, o],
            dst_ref=col_in.at[1, o],
            send_sem=sib_send.at[o],
            recv_sem=sib_recv.at[o],
            device_id=(sibling, z),
            device_id_type=MESH,
        )

    def part_copy(k):
        return pltpu.make_async_remote_copy(
            src_ref=part.at[k],
            dst_ref=part_in.at[k],
            send_sem=part_send.at[k],
            recv_sem=part_recv.at[k],
            device_id=(r, (z + (cols_n - k if k % 2 else k)) % cols_n),
            device_id_type=MESH,
        )

    def col_part_copy(b, o):
        dx, dy = offsets[o]
        dst = slot_of((-dx, -dy))
        return pltpu.make_async_remote_copy(
            src_ref=col_part.at[b, o],
            dst_ref=col_part_in.at[b, dst],
            send_sem=cp_send.at[b, o],
            recv_sem=cp_recv.at[b, dst],
            device_id=(device_at((dx, dy), b == 1), z),
            device_id_type=MESH,
        )

    row_copy(0, 1, 1).start()
    row_copy(0, 2, -2).start()
    sib_copy(0).start()
    for offset in near + diagonal:
        col_copy((0, 0), offset).start()

    def turn(pts):
        high, low = split(pts * (2.0 * scale))
        stacked = jnp.concatenate([high, low, high, low], axis=0)
        return stacked, jnp.broadcast_to(scale * jnp.sum(pts * pts, axis=0, keepdims=True), (8, block))

    def make_weights(p):
        for half in range(2):
            k = 2 * p + 1 + half
            lanes = slice(half * block, (half + 1) * block)
            weights[p, :, lanes], row_sq[p, :, lanes] = turn(row_in[k, 0:block, :])
            if k < 8:
                high, low = split(row_in[k, block : block + rhs, :])
            else:
                high = low = jnp.zeros((rhs, block), bf16)
            row_dirs[p, 0:rhs, lanes] = high
            row_dirs[p, rhs : 2 * rhs, lanes] = low

    def make_stream(b, o):
        place = pl.ds(pl.multiple_of((2 * o + b) * block, block), block)
        pts = col_in[b, o, 0:block, :]
        high, low = split(pts)
        stream[place, 0 * block : 1 * block] = high
        stream[place, 1 * block : 2 * block] = high
        stream[place, 2 * block : 3 * block] = low
        stream[place, 3 * block : 4 * block] = low
        col_sq[place, :] = jnp.broadcast_to(scale * jnp.sum(pts * pts, axis=1, keepdims=True), (block, block))
        high, low = split(col_in[b, o, block : block + rhs, :])
        dirs[0:rhs, place] = high
        dirs[rhs : 2 * rhs, place] = low

    def take_columns(arrived):
        for offset in arrived:
            col_copy((0, 0), offset).wait_recv()
            for step in relays.get(offset, ()):
                col_copy(offset, step).start()
            sib_copy(slot_of(offset)).start()

    def use_columns(c):
        for o in range(4 * c, 4 * c + 4):
            make_stream(0, o)
        for o in range(4 * c, 4 * c + 4):
            sib_copy(o).wait_recv()
        for o in range(4 * c, 4 * c + 4):
            make_stream(1, o)

    def take_row(k):
        row_copy(0, k, 0).wait_recv()
        if k + 2 < held:
            row_copy(k, k + 2, 2 if k % 2 else -2).start()

    def event_0():
        take_row(1)
        take_columns(near)
        take_row(2)
        make_weights(0)
        use_columns(0)

    def event_1():
        take_columns(diagonal)
        take_row(3)
        use_columns(1)

    def event_2():
        take_row(4)
        make_weights(1)

    def event_4():
        own_units(0)
        take_columns(far)
        take_row(5)
        use_columns(2)

    def event_5():
        use_columns(3)

    def event_6():
        take_row(6)

    def event_8():
        make_weights(2)

    def event_12():
        take_row(7)
        take_row(8)
        make_weights(3)

    events = {1: event_1, 2: event_2, 4: event_4, 5: event_5, 6: event_6, 8: event_8, 12: event_12}

    def send_rows(p):
        both = row_total[p]
        both = both[0:rhs] + both[rhs : 2 * rhs]
        for half in range(2):
            k = 2 * p + 1 + half
            part[k] = both[:, half * block : (half + 1) * block]
            part_copy(k).start()

    def send_columns(c):
        for o in range(4 * c, 4 * c + 4):
            for b in range(2):
                place = slice((2 * o + b) * block, (2 * o + b + 1) * block)
                col_part[b, o] = col_total[0:rhs, place] + col_total[rhs : 2 * rhs, place]
                if (b, o) != (0, 0):
                    col_part_copy(b, o).start()

    def finish_15():
        send_rows(3)
        send_columns(3)

    finishes = {
        5: lambda: send_rows(1),
        7: lambda: send_rows(0),
        11: lambda: send_rows(2),
        12: lambda: send_columns(0),
        13: lambda: send_columns(1),
        14: lambda: send_columns(2),
        15: finish_15,
    }

    def unit(u):
        return lookup([p for p, _ in units], u), lookup([c for _, c in units], u)

    def run(table, u, parity):
        for when, event in table.items():
            if when % 2 == parity:
                pl.when(u == when)(event)

    def products(u, tile):
        p, c = unit(u)
        place = pl.ds(pl.multiple_of(c * chunk, chunk), chunk)
        tile[...] = dot(stream[place, :], weights[p])

    def apply(u, tile):
        p, c = unit(u)
        place = pl.ds(pl.multiple_of(c * chunk, chunk), chunk)
        sq = col_sq[place, :]
        exponent = tile[...] - jnp.concatenate([sq, sq], axis=1) - row_sq[p, 0:1, :]
        high, low = split(jnp.exp2(exponent))
        row_total[p] += dot(dirs[:, place], high) + dot(dirs[:, place], low)
        col_total[:, place] += dot_turned(row_dirs[p], high) + dot_turned(row_dirs[p], low)

    own_weights[...], own_sq[...] = turn(row_in[0, 0:block, :])

    def own_products(c, tile):
        place = pl.ds(c * chunk, chunk)
        tile[...] = dot(stream[place, :], own_weights[...])

    def own_apply(c, tile):
        place = pl.ds(c * chunk, chunk)
        high, low = split(jnp.exp2(tile[...] - col_sq[place, :] - own_sq[0:1, :]))
        own_total[...] += dot(dirs[:, place], high) + dot(dirs[:, place], low)

    def own_units(c):
        own_products(c, own_a)
        own_products(c + 1, own_b)
        own_apply(c, own_a)
        own_apply(c + 1, own_b)

    event_0()
    products(0, tile_a)

    @pl.loop(0, len(units) // 2)
    def _(w):
        u = 2 * w
        run(events, u + 1, 1)
        products(u + 1, tile_b)
        apply(u, tile_a)
        run(finishes, u, 0)
        run(events, u + 2, 0)
        products(jnp.minimum(u + 2, len(units) - 1), tile_a)
        apply(u + 1, tile_b)
        run(finishes, u + 1, 1)

    own_units(2)

    direction = row_in[0, block : block + rhs, :]
    residual = res_ref[...]
    applied = own_total[0:rhs] + own_total[rhs : 2 * rhs] + col_part[0, 0] + noise_var * direction
    for k in range(8, 0, -1):
        part_copy(k).wait_recv()
        applied = applied + part_in[k]
    for o in range(plane):
        for b in range(2):
            if (b, o) != (0, 0):
                col_part_copy(b, o).wait_recv()
                applied = applied + col_part_in[b, slot_of((-offsets[o][0], -offsets[o][1]))]

    lane = lax.broadcasted_iota(jnp.int32, (rhs, block), 1)
    line = lax.broadcasted_iota(jnp.int32, (rhs, block), 0)
    packed = jnp.zeros((rhs, block), f32)
    for q, values in enumerate((residual * residual, direction * applied, residual * applied, applied * applied)):
        packed = jnp.where(lane == line + q * rhs, jnp.sum(values, axis=1, keepdims=True), packed)
    stat_z[0] = jnp.sum(packed, axis=0, keepdims=True)

    def z_copy(step):
        return pltpu.make_async_remote_copy(
            src_ref=stat_z.at[0],
            dst_ref=stat_z.at[step],
            send_sem=sz_send.at[step],
            recv_sem=sz_recv.at[step],
            device_id=(r, (z + step) % cols_n),
            device_id_type=MESH,
        )

    def r_copy(step):
        return pltpu.make_async_remote_copy(
            src_ref=stat_r.at[0],
            dst_ref=stat_r.at[step],
            send_sem=sr_send.at[step],
            recv_sem=sr_recv.at[step],
            device_id=((r + step) % rows_n, z),
            device_id_type=MESH,
        )

    for step in sorted(range(1, cols_n), key=lambda step: -min(step, cols_n - step)):
        z_copy(step).start()
    for step in range(1, cols_n):
        z_copy(step).wait_recv()
    stat_r[0] = jnp.sum(stat_z[...], axis=0)
    for step in range(1, rows_n):
        r_copy(step).start()
    for step in range(1, rows_n):
        r_copy(step).wait_recv()
    sums = jnp.broadcast_to(jnp.sum(stat_r[...], axis=0), (rhs, block))

    def take(q):
        return jnp.sum(jnp.where(lane == line + q * rhs, sums, 0.0), axis=1, keepdims=True)

    norm_now, curvature, cross, square = take(0), take(1), take(2), take(3)
    step_size = norm_now / curvature
    norm_next = jnp.maximum(norm_now - step_size * (2.0 * cross - step_size * square), 0.0)
    ratio = norm_next / norm_now
    next_residual = residual - step_size * applied
    nsol_ref[...] = sol_ref[...] + step_size * direction
    nres_ref[...] = next_residual
    ndir_ref[...] = next_residual + ratio * direction

    for k in range(1, held):
        row_copy(0, k, 0).wait_send()
        part_copy(k).wait_send()
    for step in range(1, cols_n):
        z_copy(step).wait_send()
    for step in range(1, rows_n):
        r_copy(step).wait_send()
    for o in range(plane):
        sib_copy(o).wait_send()
        if o > 0:
            col_copy((0, 0), offsets[o]).wait_send()
        for b in range(2):
            if (b, o) != (0, 0):
                col_part_copy(b, o).wait_send()


def per_device(points, solution, residual, direction):
    vmem = pl.BlockSpec(memory_space=pltpu.VMEM)
    dma = pltpu.SemaphoreType.DMA
    out = jax.ShapeDtypeStruct((rhs, block), f32)
    span = rows_n * block
    return pl.pallas_call(
        kernel,
        out_shape=(out, out, out),
        in_specs=[pl.BlockSpec(memory_space=pltpu.HBM)] * 4,
        out_specs=(vmem, vmem, vmem),
        scratch_shapes=[
            pltpu.VMEM((2, plane, block + rhs, block), f32),
            pltpu.VMEM((held, block + rhs, block), f32),
            pltpu.VMEM((pairs, 4 * block, 2 * block), bf16),
            pltpu.VMEM((pairs, 8, 2 * block), f32),
            pltpu.VMEM((pairs, 2 * rhs, 2 * block), bf16),
            pltpu.VMEM((span, 4 * block), bf16),
            pltpu.VMEM((span, block), f32),
            pltpu.VMEM((2 * rhs, span), bf16),
            pltpu.VMEM((4 * block, block), bf16),
            pltpu.VMEM((8, block), f32),
            pltpu.VMEM((chunk, 2 * block), f32),
            pltpu.VMEM((chunk, 2 * block), f32),
            pltpu.VMEM((chunk, block), f32),
            pltpu.VMEM((chunk, block), f32),
            pltpu.VMEM((pairs, 2 * rhs, 2 * block), f32),
            pltpu.VMEM((2 * rhs, span), f32),
            pltpu.VMEM((2 * rhs, block), f32),
            pltpu.VMEM((held, rhs, block), f32),
            pltpu.VMEM((held, rhs, block), f32),
            pltpu.VMEM((2, plane, rhs, block), f32),
            pltpu.VMEM((2, plane, rhs, block), f32),
            pltpu.VMEM((cols_n, 1, block), f32),
            pltpu.VMEM((rows_n, 1, block), f32),
            pltpu.VMEM((rhs, block), f32),
            pltpu.VMEM((rhs, block), f32),
            dma((4,)),
            dma((plane,)),
            dma((plane,)),
            dma((plane,)),
            dma((plane,)),
            dma((held,)),
            dma((held,)),
            dma((held,)),
            dma((held,)),
            dma((2, plane)),
            dma((2, plane)),
            dma((cols_n,)),
            dma((cols_n,)),
            dma((rows_n,)),
            dma((rows_n,)),
        ],
        compiler_params=pltpu.CompilerParams(
            collective_id=0, has_side_effects=True, vmem_limit_bytes=60 * 1024 * 1024
        ),
        name="cg_step",
    )(points, solution, residual, direction)


def solution(mesh):
    spec = P(None, ("row", "col"))
    return jax.shard_map(
        per_device, mesh=mesh, in_specs=(spec,) * 4, out_specs=(spec,) * 3, check_vma=False
    )
```

```python
import math

import jax
import jax.numpy as jnp
from jax import lax
from jax.experimental import pallas as pl
from jax.experimental.pallas import tpu as pltpu
from jax.sharding import PartitionSpec as P

noise_var = 0.5
inv_two_len = 0.03125
scale = inv_two_len * math.log2(math.e)

MESH = pl.DeviceIdType.MESH
f32 = jnp.float32
bf16 = jnp.bfloat16

side = 4
rows_n = 32
cols_n = 16
block = 128
rhs = 16
chunk = 1024
chunks = 4
pairs = 4
held = 9
half_rows = (block + rhs) // 2

offsets = [
    (0, 0), (1, 0), (3, 0), (0, 1),
    (0, 3), (1, 1), (3, 3), (1, 3),
    (3, 1), (2, 0), (0, 2), (2, 1),
    (2, 3), (3, 2), (1, 2), (2, 2),
]
plane = len(offsets)
near = [(1, 0), (3, 0), (0, 1), (0, 3)]
diagonal = [(1, 1), (3, 3), (3, 1), (1, 3)]
far = [o for o in offsets if o not in near + diagonal + [(0, 0)]]
relays = {
    (3, 0): [(3, 0)],
    (0, 3): [(0, 3)],
    (1, 1): [(1, 0), (1, 1)],
    (3, 3): [(3, 0)],
    (3, 1): [(0, 1)],
    (1, 3): [(0, 3)],
}

def slot_of(offset):
    return offsets.index((offset[0] % side, offset[1] % side))


def split(values):
    high = values.astype(bf16)
    low = (values - high.astype(f32)).astype(bf16)
    return high, low


def dot(a, b):
    return jnp.dot(a, b, preferred_element_type=f32)


def dot_turned(a, b):
    return lax.dot_general(a, b, (((1,), (1,)), ((), ())), preferred_element_type=f32)


def kernel(
    pts_hbm,
    res_hbm,
    dir_hbm,
    applied_ref,
    step_ref,
    ratio_ref,
    col_in,
    row_in,
    weights,
    row_sq,
    row_dirs,
    stream,
    col_sq,
    dirs,
    own_weights,
    own_sq,
    tile_a,
    tile_b,
    own_a,
    own_b,
    row_total,
    col_total,
    own_total,
    part,
    part_in,
    col_part,
    col_part_in,
    stat_z,
    stat_r,
    res_ref,
    load,
    col_send,
    col_recv,
    sib_send,
    sib_recv,
    row_send,
    row_recv,
    part_send,
    part_recv,
    cp_send,
    cp_recv,
    sz_send,
    sz_recv,
    sr_send,
    sr_recv,
):
    r = lax.axis_index("row")
    z = lax.axis_index("col")
    x, y, core = r // 8, (r // 2) % 4, r % 2
    sibling = r + 1 - 2 * core

    def device_at(offset, other):
        target = (((x + offset[0]) % side) * side + (y + offset[1]) % side) * 2
        return target + (1 - core if other else core)

    loads = [
        pltpu.make_async_copy(src, dst, load.at[i])
        for i, (src, dst) in enumerate(
            (
                (pts_hbm, row_in.at[0, 0:block]),
                (dir_hbm, row_in.at[0, block : block + rhs]),
                (res_hbm, res_ref),
            )
        )
    ]
    for copy in loads:
        copy.start()

    barrier = pltpu.get_barrier_semaphore()
    for step in (2, 14, 1, 15):
        pl.semaphore_signal(barrier, inc=1, device_id=(r, (z + step) % cols_n), device_id_type=MESH)
    for offset in diagonal + near:
        pl.semaphore_signal(barrier, inc=1, device_id=(device_at(offset, False), z), device_id_type=MESH)
    pl.semaphore_signal(barrier, inc=1, device_id=(sibling, z), device_id_type=MESH)

    for copy in loads:
        copy.wait()
    col_in[0, 0, 0:block, :] = row_in[0, 0:block, :].T
    col_in[0, 0, block : block + rhs, :] = row_in[0, block : block + rhs, :]
    row_total[...] = jnp.zeros_like(row_total)
    col_total[...] = jnp.zeros_like(col_total)
    own_total[...] = jnp.zeros_like(own_total)

    pl.semaphore_wait(barrier, 13)

    def row_copy(src, dst, half, step):
        place = pl.ds(half * half_rows, half_rows)
        return pltpu.make_async_remote_copy(
            src_ref=row_in.at[src, place],
            dst_ref=row_in.at[dst, place],
            send_sem=row_send.at[dst, half],
            recv_sem=row_recv.at[dst, half],
            device_id=(r, (z + cols_n + step) % cols_n),
            device_id_type=MESH,
        )

    def col_copy(offset, step):
        dst = slot_of((offset[0] + step[0], offset[1] + step[1]))
        return pltpu.make_async_remote_copy(
            src_ref=col_in.at[0, slot_of(offset)],
            dst_ref=col_in.at[0, dst],
            send_sem=col_send.at[dst],
            recv_sem=col_recv.at[dst],
            device_id=(device_at((side - step[0], side - step[1]), False), z),
            device_id_type=MESH,
        )

    def sib_copy(o):
        return pltpu.make_async_remote_copy(
            src_ref=col_in.at[0, o],
            dst_ref=col_in.at[1, o],
            send_sem=sib_send.at[o],
            recv_sem=sib_recv.at[o],
            device_id=(sibling, z),
            device_id_type=MESH,
        )

    def part_copy(k):
        return pltpu.make_async_remote_copy(
            src_ref=part.at[k],
            dst_ref=part_in.at[k],
            send_sem=part_send.at[k],
            recv_sem=part_recv.at[k],
            device_id=(r, (z + (cols_n - k if k % 2 else k)) % cols_n),
            device_id_type=MESH,
        )

    def col_part_copy(b, o):
        dx, dy = offsets[o]
        dst = slot_of((-dx, -dy))
        return pltpu.make_async_remote_copy(
            src_ref=col_part.at[b, o],
            dst_ref=col_part_in.at[b, dst],
            send_sem=cp_send.at[b, o],
            recv_sem=cp_recv.at[b, dst],
            device_id=(device_at((dx, dy), b == 1), z),
            device_id_type=MESH,
        )

    for half in range(2):
        row_copy(0, 1, half, 1).start()
        row_copy(0, 2, half, -2).start()
    sib_copy(0).start()
    for offset in near + diagonal:
        col_copy((0, 0), offset).start()

    def turn(pts):
        high, low = split(pts * (2.0 * scale))
        stacked = jnp.concatenate([high, low, high, low], axis=0)
        return stacked, jnp.broadcast_to(scale * jnp.sum(pts * pts, axis=0, keepdims=True), (8, block))

    def make_weights(p):
        for half in range(2):
            k = 2 * p + 1 + half
            lanes = slice(half * block, (half + 1) * block)
            weights[p, :, lanes], row_sq[p, :, lanes] = turn(row_in[k, 0:block, :])
            if k < 8:
                high, low = split(row_in[k, block : block + rhs, :])
            else:
                high = low = jnp.zeros((rhs, block), bf16)
            row_dirs[p, 0:rhs, lanes] = high
            row_dirs[p, rhs : 2 * rhs, lanes] = low

    def make_stream(b, o):
        place = pl.ds(pl.multiple_of((2 * o + b) * block, block), block)
        pts = col_in[b, o, 0:block, :]
        high, low = split(pts)
        stream[place, 0 * block : 1 * block] = high
        stream[place, 1 * block : 2 * block] = high
        stream[place, 2 * block : 3 * block] = low
        stream[place, 3 * block : 4 * block] = low
        col_sq[place, :] = jnp.broadcast_to(scale * jnp.sum(pts * pts, axis=1, keepdims=True), (block, block))
        high, low = split(col_in[b, o, block : block + rhs, :])
        dirs[0:rhs, place] = high
        dirs[rhs : 2 * rhs, place] = low

    def take_columns(arrived):
        for offset in arrived:
            col_copy((0, 0), offset).wait_recv()
            for step in relays.get(offset, ()):
                col_copy(offset, step).start()
            sib_copy(slot_of(offset)).start()

    def use_columns(c):
        for o in range(4 * c, 4 * c + 4):
            make_stream(0, o)
        for o in range(4 * c, 4 * c + 4):
            sib_copy(o).wait_recv()
        for o in range(4 * c, 4 * c + 4):
            make_stream(1, o)

    def take_row(k, half):
        row_copy(0, k, half, 0).wait_recv()
        if k + 2 < held:
            row_copy(k, k + 2, half, 2 if k % 2 else -2).start()

    def send_rows(p):
        both = row_total[p]
        both = both[0:rhs] + both[rhs : 2 * rhs]
        for half in range(2):
            k = 2 * p + 1 + half
            part[k] = both[:, half * block : (half + 1) * block]
            part_copy(k).start()

    def send_columns(c):
        for o in range(4 * c, 4 * c + 4):
            for b in range(2):
                place = slice((2 * o + b) * block, (2 * o + b + 1) * block)
                col_part[b, o] = col_total[0:rhs, place] + col_total[rhs : 2 * rhs, place]
                if (b, o) != (0, 0):
                    col_part_copy(b, o).start()

    def products(p, c, tile):
        place = pl.ds(c * chunk, chunk)
        tile[...] = dot(stream[place, :], weights[p])

    def apply(p, c, tile):
        place = pl.ds(c * chunk, chunk)
        sq = col_sq[place, :]
        exponent = tile[...] - jnp.concatenate([sq, sq], axis=1) - row_sq[p, 0:1, :]
        high, low = split(jnp.exp2(exponent))
        row_total[p] += dot(dirs[:, place], high) + dot(dirs[:, place], low)
        col_total[:, place] += dot_turned(row_dirs[p], high) + dot_turned(row_dirs[p], low)

    own_weights[...], own_sq[...] = turn(row_in[0, 0:block, :])

    def own_products(c, tile):
        place = pl.ds(c * chunk, chunk)
        tile[...] = dot(stream[place, :], own_weights[...])

    def own_apply(c, tile):
        place = pl.ds(c * chunk, chunk)
        high, low = split(jnp.exp2(tile[...] - col_sq[place, :] - own_sq[0:1, :]))
        own_total[...] += dot(dirs[:, place], high) + dot(dirs[:, place], low)

    waiting = []

    def flush():
        while waiting:
            waiting.pop()()

    def unit(p, c, tile):
        products(p, c, tile)
        flush()
        waiting.append(lambda: apply(p, c, tile))

    def own(c, tile):
        own_products(c, tile)
        flush()
        waiting.append(lambda: own_apply(c, tile))

    take_row(1, 0)
    take_row(1, 1)
    take_row(2, 0)
    take_columns(near)
    take_row(2, 1)
    make_weights(0)
    use_columns(0)
    unit(0, 0, tile_a)
    own(0, own_a)
    flush()
    take_row(3, 0)
    take_columns(diagonal)
    take_row(4, 0)
    take_row(3, 1)
    use_columns(1)
    unit(0, 1, tile_b)
    flush()
    take_row(4, 1)
    make_weights(1)
    unit(1, 0, tile_a)
    own(1, own_b)
    unit(1, 1, tile_b)
    flush()
    take_row(5, 0)
    take_columns(far)
    take_row(6, 0)
    take_row(5, 1)
    use_columns(2)
    unit(0, 2, tile_a)
    take_row(6, 1)
    make_weights(2)
    unit(1, 2, tile_b)
    use_columns(3)
    unit(0, 3, tile_a)
    unit(1, 3, tile_b)
    send_rows(0)
    unit(2, 2, tile_a)
    send_rows(1)
    unit(2, 3, tile_b)
    flush()
    for half in range(2):
        take_row(7, half)
        take_row(8, half)
    make_weights(3)
    unit(3, 3, tile_a)
    unit(3, 2, tile_b)
    send_columns(3)
    unit(3, 1, tile_a)
    send_columns(2)
    unit(3, 0, tile_b)
    unit(2, 1, tile_a)
    send_rows(3)
    unit(2, 0, tile_b)
    send_columns(1)
    own(2, own_a)
    send_rows(2)
    send_columns(0)
    own(3, own_b)
    flush()

    direction = row_in[0, block : block + rhs, :]
    residual = res_ref[...]
    applied = own_total[0:rhs] + own_total[rhs : 2 * rhs] + col_part[0, 0] + noise_var * direction
    for k in range(8, 0, -1):
        part_copy(k).wait_recv()
        applied = applied + part_in[k]
    for o in range(plane):
        for b in range(2):
            if (b, o) != (0, 0):
                col_part_copy(b, o).wait_recv()
                applied = applied + col_part_in[b, slot_of((-offsets[o][0], -offsets[o][1]))]

    lane = lax.broadcasted_iota(jnp.int32, (rhs, block), 1)
    line = lax.broadcasted_iota(jnp.int32, (rhs, block), 0)
    packed = jnp.zeros((rhs, block), f32)
    for q, values in enumerate((residual * residual, direction * applied, residual * applied, applied * applied)):
        packed = jnp.where(lane == line + q * rhs, jnp.sum(values, axis=1, keepdims=True), packed)
    stat_z[0] = jnp.sum(packed, axis=0, keepdims=True)

    def z_copy(step):
        return pltpu.make_async_remote_copy(
            src_ref=stat_z.at[0],
            dst_ref=stat_z.at[step],
            send_sem=sz_send.at[step],
            recv_sem=sz_recv.at[step],
            device_id=(r, (z + step) % cols_n),
            device_id_type=MESH,
        )

    def r_copy(b, o):
        dx, dy = offsets[o]
        dst = 2 * slot_of((-dx, -dy)) + b
        return pltpu.make_async_remote_copy(
            src_ref=stat_r.at[0],
            dst_ref=stat_r.at[dst],
            send_sem=sr_send.at[2 * o + b],
            recv_sem=sr_recv.at[dst],
            device_id=(device_at((dx, dy), b == 1), z),
            device_id_type=MESH,
        )

    others = [(b, o) for o in range(plane - 1, -1, -1) for b in range(2) if (b, o) != (0, 0)]
    for step in sorted(range(1, cols_n), key=lambda step: -min(step, cols_n - step)):
        z_copy(step).start()
    for step in range(1, cols_n):
        z_copy(step).wait_recv()
    stat_r[0] = jnp.sum(stat_z[...], axis=0)
    for b, o in others:
        r_copy(b, o).start()
    for b, o in others:
        r_copy(b, o).wait_recv()
    sums = jnp.broadcast_to(jnp.sum(stat_r[...], axis=0), (rhs, block))

    def take(q):
        return jnp.sum(jnp.where(lane == line + q * rhs, sums, 0.0), axis=1, keepdims=True)

    norm_now, curvature, cross, square = take(0), take(1), take(2), take(3)
    step_size = norm_now / curvature
    norm_next = jnp.maximum(norm_now - step_size * (2.0 * cross - step_size * square), 0.0)
    ratio = norm_next / norm_now
    applied_ref[...] = applied
    step_ref[...] = jnp.broadcast_to(step_size, (rhs, block))
    ratio_ref[...] = jnp.broadcast_to(ratio, (rhs, block))

    for k in range(1, held):
        for half in range(2):
            row_copy(0, k, half, 0).wait_send()
        part_copy(k).wait_send()
    for step in range(1, cols_n):
        z_copy(step).wait_send()
    for b, o in others:
        r_copy(b, o).wait_send()
    for o in range(plane):
        sib_copy(o).wait_send()
        if o > 0:
            col_copy((0, 0), offsets[o]).wait_send()
        for b in range(2):
            if (b, o) != (0, 0):
                col_part_copy(b, o).wait_send()


def per_device(points, solution, residual, direction):
    vmem = pl.BlockSpec(memory_space=pltpu.VMEM)
    dma = pltpu.SemaphoreType.DMA
    out = jax.ShapeDtypeStruct((rhs, block), f32)
    span = rows_n * block
    applied, step_size, ratio = pl.pallas_call(
        kernel,
        out_shape=(out, out, out),
        in_specs=[pl.BlockSpec(memory_space=pltpu.HBM)] * 3,
        out_specs=(vmem, vmem, vmem),
        scratch_shapes=[
            pltpu.VMEM((2, plane, block + rhs, block), f32),
            pltpu.VMEM((held, block + rhs, block), f32),
            pltpu.VMEM((pairs, 4 * block, 2 * block), bf16),
            pltpu.VMEM((pairs, 8, 2 * block), f32),
            pltpu.VMEM((pairs, 2 * rhs, 2 * block), bf16),
            pltpu.VMEM((span, 4 * block), bf16),
            pltpu.VMEM((span, block), f32),
            pltpu.VMEM((2 * rhs, span), bf16),
            pltpu.VMEM((4 * block, block), bf16),
            pltpu.VMEM((8, block), f32),
            pltpu.VMEM((chunk, 2 * block), f32),
            pltpu.VMEM((chunk, 2 * block), f32),
            pltpu.VMEM((chunk, block), f32),
            pltpu.VMEM((chunk, block), f32),
            pltpu.VMEM((pairs, 2 * rhs, 2 * block), f32),
            pltpu.VMEM((2 * rhs, span), f32),
            pltpu.VMEM((2 * rhs, block), f32),
            pltpu.VMEM((held, rhs, block), f32),
            pltpu.VMEM((held, rhs, block), f32),
            pltpu.VMEM((2, plane, rhs, block), f32),
            pltpu.VMEM((2, plane, rhs, block), f32),
            pltpu.VMEM((cols_n, 1, block), f32),
            pltpu.VMEM((rows_n, 1, block), f32),
            pltpu.VMEM((rhs, block), f32),
            dma((3,)),
            dma((plane,)),
            dma((plane,)),
            dma((plane,)),
            dma((plane,)),
            dma((held, 2)),
            dma((held, 2)),
            dma((held,)),
            dma((held,)),
            dma((2, plane)),
            dma((2, plane)),
            dma((cols_n,)),
            dma((cols_n,)),
            dma((rows_n,)),
            dma((rows_n,)),
        ],
        compiler_params=pltpu.CompilerParams(
            collective_id=0, has_side_effects=True, vmem_limit_bytes=60 * 1024 * 1024
        ),
        name="cg_step",
    )(points, residual, direction)
    next_residual = residual - step_size * applied
    return solution + step_size * direction, next_residual, next_residual + ratio * direction


def solution(mesh):
    spec = P(None, ("row", "col"))
    return jax.shard_map(
        per_device, mesh=mesh, in_specs=(spec,) * 4, out_specs=(spec,) * 3, check_vma=False
    )
```

```python
import math

import jax
import jax.numpy as jnp
from jax import lax
from jax.experimental import pallas as pl
from jax.experimental.pallas import tpu as pltpu
from jax.sharding import PartitionSpec as P

noise_var = 0.5
inv_two_len = 0.03125
scale = inv_two_len * math.log2(math.e)

MESH = pl.DeviceIdType.MESH
f32 = jnp.float32
bf16 = jnp.bfloat16

side = 4
rows_n = 32
cols_n = 16
block = 128
rhs = 16
chunk = 1024
chunks = 4
pairs = 4
held = 9
half_rows = (block + rhs) // 2

offsets = [
    (0, 0), (1, 0), (3, 0), (0, 1),
    (0, 3), (1, 1), (3, 3), (1, 3),
    (3, 1), (2, 0), (0, 2), (2, 1),
    (2, 3), (3, 2), (1, 2), (2, 2),
]
plane = len(offsets)
near = [(1, 0), (3, 0), (0, 1), (0, 3)]
diagonal = [(1, 1), (3, 3), (3, 1), (1, 3)]
far = [o for o in offsets if o not in near + diagonal + [(0, 0)]]
relays = {
    (3, 0): [(3, 0)],
    (0, 3): [(0, 3)],
    (1, 1): [(1, 0), (1, 1)],
    (3, 3): [(3, 0)],
    (3, 1): [(0, 1)],
    (1, 3): [(0, 3)],
}

def slot_of(offset):
    return offsets.index((offset[0] % side, offset[1] % side))


def split(values):
    high = values.astype(bf16)
    low = (values - high.astype(f32)).astype(bf16)
    return high, low


def dot(a, b):
    return jnp.dot(a, b, preferred_element_type=f32)


def dot_turned(a, b):
    return lax.dot_general(a, b, (((1,), (1,)), ((), ())), preferred_element_type=f32)


def kernel(
    pts_hbm,
    res_hbm,
    dir_hbm,
    applied_ref,
    step_ref,
    ratio_ref,
    col_in,
    row_in,
    weights,
    row_sq,
    row_dirs,
    stream,
    col_sq,
    dirs,
    own_weights,
    own_sq,
    tile_a,
    tile_b,
    own_a,
    own_b,
    kept,
    row_total,
    col_total,
    own_total,
    part,
    part_in,
    col_part,
    col_part_in,
    stat_z,
    stat_r,
    res_ref,
    load,
    col_send,
    col_recv,
    sib_send,
    sib_recv,
    row_send,
    row_recv,
    part_send,
    part_recv,
    cp_send,
    cp_recv,
    sz_send,
    sz_recv,
    sr_send,
    sr_recv,
):
    r = lax.axis_index("row")
    z = lax.axis_index("col")
    x, y, core = r // 8, (r // 2) % 4, r % 2
    sibling = r + 1 - 2 * core

    def device_at(offset, other):
        target = (((x + offset[0]) % side) * side + (y + offset[1]) % side) * 2
        return target + (1 - core if other else core)

    loads = [
        pltpu.make_async_copy(src, dst, load.at[i])
        for i, (src, dst) in enumerate(
            (
                (pts_hbm, row_in.at[0, 0:block]),
                (dir_hbm, row_in.at[0, block : block + rhs]),
                (res_hbm, res_ref),
            )
        )
    ]
    for copy in loads:
        copy.start()

    barrier = pltpu.get_barrier_semaphore()
    for step in (2, 14, 1, 15):
        pl.semaphore_signal(barrier, inc=1, device_id=(r, (z + step) % cols_n), device_id_type=MESH)
    for offset in diagonal + near:
        pl.semaphore_signal(barrier, inc=1, device_id=(device_at(offset, False), z), device_id_type=MESH)
    pl.semaphore_signal(barrier, inc=1, device_id=(sibling, z), device_id_type=MESH)

    for copy in loads:
        copy.wait()
    col_in[0, 0, 0:block, :] = row_in[0, 0:block, :].T
    col_in[0, 0, block : block + rhs, :] = row_in[0, block : block + rhs, :]
    row_total[...] = jnp.zeros_like(row_total)
    col_total[...] = jnp.zeros_like(col_total)
    own_total[...] = jnp.zeros_like(own_total)

    pl.semaphore_wait(barrier, 13)

    def row_copy(src, dst, half, step):
        place = pl.ds(half * half_rows, half_rows)
        return pltpu.make_async_remote_copy(
            src_ref=row_in.at[src, place],
            dst_ref=row_in.at[dst, place],
            send_sem=row_send.at[dst, half],
            recv_sem=row_recv.at[dst, half],
            device_id=(r, (z + cols_n + step) % cols_n),
            device_id_type=MESH,
        )

    def col_copy(offset, step):
        dst = slot_of((offset[0] + step[0], offset[1] + step[1]))
        return pltpu.make_async_remote_copy(
            src_ref=col_in.at[0, slot_of(offset)],
            dst_ref=col_in.at[0, dst],
            send_sem=col_send.at[dst],
            recv_sem=col_recv.at[dst],
            device_id=(device_at((side - step[0], side - step[1]), False), z),
            device_id_type=MESH,
        )

    def sib_copy(o):
        return pltpu.make_async_remote_copy(
            src_ref=col_in.at[0, o],
            dst_ref=col_in.at[1, o],
            send_sem=sib_send.at[o],
            recv_sem=sib_recv.at[o],
            device_id=(sibling, z),
            device_id_type=MESH,
        )

    def part_copy(k):
        return pltpu.make_async_remote_copy(
            src_ref=part.at[k],
            dst_ref=part_in.at[k],
            send_sem=part_send.at[k],
            recv_sem=part_recv.at[k],
            device_id=(r, (z + (cols_n - k if k % 2 else k)) % cols_n),
            device_id_type=MESH,
        )

    def col_part_copy(b, o):
        dx, dy = offsets[o]
        dst = slot_of((-dx, -dy))
        return pltpu.make_async_remote_copy(
            src_ref=col_part.at[b, o],
            dst_ref=col_part_in.at[b, dst],
            send_sem=cp_send.at[b, o],
            recv_sem=cp_recv.at[b, dst],
            device_id=(device_at((dx, dy), b == 1), z),
            device_id_type=MESH,
        )

    for half in range(2):
        row_copy(0, 1, half, 1).start()
        row_copy(0, 2, half, -2).start()
    sib_copy(0).start()
    for offset in near + diagonal:
        col_copy((0, 0), offset).start()

    def turn(pts):
        high, low = split(pts * (2.0 * scale))
        stacked = jnp.concatenate([high, low, high, low], axis=0)
        return stacked, jnp.broadcast_to(scale * jnp.sum(pts * pts, axis=0, keepdims=True), (8, block))

    def make_weights(p):
        for half in range(2):
            k = 2 * p + 1 + half
            lanes = slice(half * block, (half + 1) * block)
            weights[p, :, lanes], row_sq[p, :, lanes] = turn(row_in[k, 0:block, :])
            if k < 8:
                high, low = split(row_in[k, block : block + rhs, :])
            else:
                high = low = jnp.zeros((rhs, block), bf16)
            row_dirs[p, 0:rhs, lanes] = high
            row_dirs[p, rhs : 2 * rhs, lanes] = low

    def make_stream(b, o):
        place = pl.ds(pl.multiple_of((2 * o + b) * block, block), block)
        pts = col_in[b, o, 0:block, :]
        high, low = split(pts)
        stream[place, 0 * block : 1 * block] = high
        stream[place, 1 * block : 2 * block] = high
        stream[place, 2 * block : 3 * block] = low
        stream[place, 3 * block : 4 * block] = low
        col_sq[place, :] = jnp.broadcast_to(scale * jnp.sum(pts * pts, axis=1, keepdims=True), (block, block))
        high, low = split(col_in[b, o, block : block + rhs, :])
        dirs[0:rhs, place] = high
        dirs[rhs : 2 * rhs, place] = low

    def take_columns(arrived):
        for offset in arrived:
            col_copy((0, 0), offset).wait_recv()
            for step in relays.get(offset, ()):
                col_copy(offset, step).start()
            sib_copy(slot_of(offset)).start()

    def use_columns(c):
        for o in range(4 * c, 4 * c + 4):
            make_stream(0, o)
        for o in range(4 * c, 4 * c + 4):
            sib_copy(o).wait_recv()
        for o in range(4 * c, 4 * c + 4):
            make_stream(1, o)

    def take_row(k, half):
        row_copy(0, k, half, 0).wait_recv()
        if k + 2 < held:
            row_copy(k, k + 2, half, 2 if k % 2 else -2).start()

    def send_rows(p):
        both = row_total[p]
        both = both[0:rhs] + both[rhs : 2 * rhs]
        for half in range(2):
            k = 2 * p + 1 + half
            part[k] = both[:, half * block : (half + 1) * block]
        for half in range(2):
            part_copy(2 * p + 1 + half).start()

    def send_columns(c):
        for o in range(4 * c, 4 * c + 4):
            for b in range(2):
                place = slice((2 * o + b) * block, (2 * o + b + 1) * block)
                col_part[b, o] = col_total[0:rhs, place] + col_total[rhs : 2 * rhs, place]
        for o in range(4 * c + 3, 4 * c - 1, -1):
            for b in range(2):
                if (b, o) != (0, 0):
                    col_part_copy(b, o).start()

    def products(p, c, tile):
        place = pl.ds(c * chunk, chunk)
        tile[...] = dot(stream[place, :], weights[p])

    def apply(p, c, tile):
        place = pl.ds(c * chunk, chunk)
        sq = col_sq[place, :]
        exponent = tile[...] - jnp.concatenate([sq, sq], axis=1) - row_sq[p, 0:1, :]
        high, low = split(jnp.exp2(exponent))
        row_total[p] += dot(dirs[:, place], high) + dot(dirs[:, place], low)
        col_total[:, place] += dot_turned(row_dirs[p], high) + dot_turned(row_dirs[p], low)

    def late_apply(c, tile):
        place = pl.ds(c * chunk, chunk)
        sq = col_sq[place, :]
        exponent = tile[...] - jnp.concatenate([sq, sq], axis=1) - row_sq[3, 0:1, :]
        high, low = split(jnp.exp2(exponent))
        kept[0, c], kept[1, c] = high, low
        row_total[3] += dot(dirs[:, place], high) + dot(dirs[:, place], low)

    def late_columns(c):
        place = pl.ds(c * chunk, chunk)
        col_total[:, place] += dot_turned(row_dirs[3], kept[0, c]) + dot_turned(row_dirs[3], kept[1, c])

    own_weights[...], own_sq[...] = turn(row_in[0, 0:block, :])

    def own_products(c, tile):
        place = pl.ds(c * chunk, chunk)
        tile[...] = dot(stream[place, :], own_weights[...])

    def own_apply(c, tile):
        place = pl.ds(c * chunk, chunk)
        high, low = split(jnp.exp2(tile[...] - col_sq[place, :] - own_sq[0:1, :]))
        own_total[...] += dot(dirs[:, place], high) + dot(dirs[:, place], low)

    waiting = []

    def flush():
        while waiting:
            waiting.pop()()

    def unit(p, c, tile):
        products(p, c, tile)
        flush()
        waiting.append(lambda: apply(p, c, tile))

    def late_unit(c, tile):
        products(3, c, tile)
        flush()
        waiting.append(lambda: late_apply(c, tile))

    def own(c, tile):
        own_products(c, tile)
        flush()
        waiting.append(lambda: own_apply(c, tile))

    take_row(1, 0)
    take_row(1, 1)
    take_row(2, 0)
    take_columns(near)
    take_row(2, 1)
    make_weights(0)
    use_columns(0)
    unit(0, 0, tile_a)
    own(0, own_a)
    flush()
    take_row(3, 0)
    take_columns(diagonal)
    take_row(4, 0)
    take_row(3, 1)
    use_columns(1)
    unit(0, 1, tile_b)
    flush()
    take_row(4, 1)
    take_columns(far[:2])
    make_weights(1)
    unit(1, 0, tile_a)
    own(1, own_b)
    flush()
    take_row(5, 0)
    take_columns(far[2:3])
    use_columns(2)
    unit(0, 2, tile_b)
    take_row(6, 0)
    take_row(5, 1)
    take_columns(far[3:])
    unit(1, 2, tile_a)
    take_row(6, 1)
    make_weights(2)
    use_columns(3)
    unit(2, 2, tile_b)
    unit(2, 0, tile_a)
    unit(2, 3, tile_b)
    unit(2, 1, tile_a)
    unit(0, 3, tile_b)
    send_rows(2)
    flush()
    send_rows(0)
    for half in range(2):
        take_row(7, half)
        take_row(8, half)
    make_weights(3)
    for c, tile in ((0, tile_a), (1, tile_b), (2, tile_a), (3, tile_b)):
        late_unit(c, tile)
    unit(1, 3, tile_a)
    send_rows(3)
    unit(1, 1, tile_b)
    late_columns(3)
    send_columns(3)
    late_columns(2)
    send_columns(2)
    own(2, own_a)
    send_rows(1)
    late_columns(1)
    send_columns(1)
    late_columns(0)
    send_columns(0)
    own(3, own_b)
    flush()

    direction = row_in[0, block : block + rhs, :]
    residual = res_ref[...]
    applied = own_total[0:rhs] + own_total[rhs : 2 * rhs] + col_part[0, 0] + noise_var * direction
    for o in range(plane):
        for b in range(2):
            if (b, o) != (0, 0):
                col_part_copy(b, o).wait_recv()
    for b in range(2):
        for o in range(plane):
            if (b, o) != (0, 0):
                applied = applied + col_part_in[b, o]
    for k in range(1, held):
        part_copy(k).wait_recv()
    for k in range(1, held):
        applied = applied + part_in[k]

    lane = lax.broadcasted_iota(jnp.int32, (rhs, block), 1)
    line = lax.broadcasted_iota(jnp.int32, (rhs, block), 0)
    packed = jnp.zeros((rhs, block), f32)
    for q, values in enumerate((residual * residual, direction * applied, residual * applied, applied * applied)):
        packed = jnp.where(lane == line + q * rhs, jnp.sum(values, axis=1, keepdims=True), packed)
    stat_z[0] = jnp.sum(packed, axis=0, keepdims=True)

    def z_copy(step):
        return pltpu.make_async_remote_copy(
            src_ref=stat_z.at[0],
            dst_ref=stat_z.at[step],
            send_sem=sz_send.at[step],
            recv_sem=sz_recv.at[step],
            device_id=(r, (z + step) % cols_n),
            device_id_type=MESH,
        )

    def r_copy(b, o):
        dx, dy = offsets[o]
        dst = 2 * slot_of((-dx, -dy)) + b
        return pltpu.make_async_remote_copy(
            src_ref=stat_r.at[0],
            dst_ref=stat_r.at[dst],
            send_sem=sr_send.at[2 * o + b],
            recv_sem=sr_recv.at[dst],
            device_id=(device_at((dx, dy), b == 1), z),
            device_id_type=MESH,
        )

    others = [(b, o) for o in range(plane - 1, -1, -1) for b in range(2) if (b, o) != (0, 0)]
    for step in sorted(range(1, cols_n), key=lambda step: -min(step, cols_n - step)):
        z_copy(step).start()
    for step in range(1, cols_n):
        z_copy(step).wait_recv()
    stat_r[0] = jnp.sum(stat_z[...], axis=0)
    for b, o in others:
        r_copy(b, o).start()
    for b, o in others:
        r_copy(b, o).wait_recv()
    sums = jnp.broadcast_to(jnp.sum(stat_r[...], axis=0), (rhs, block))

    def take(q):
        return jnp.sum(jnp.where(lane == line + q * rhs, sums, 0.0), axis=1, keepdims=True)

    norm_now, curvature, cross, square = take(0), take(1), take(2), take(3)
    step_size = norm_now / curvature
    norm_next = jnp.maximum(norm_now - step_size * (2.0 * cross - step_size * square), 0.0)
    ratio = norm_next / norm_now
    applied_ref[...] = applied
    step_ref[...] = jnp.broadcast_to(step_size, (rhs, block))
    ratio_ref[...] = jnp.broadcast_to(ratio, (rhs, block))

    for k in range(1, held):
        for half in range(2):
            row_copy(0, k, half, 0).wait_send()
        part_copy(k).wait_send()
    for step in range(1, cols_n):
        z_copy(step).wait_send()
    for b, o in others:
        r_copy(b, o).wait_send()
    for o in range(plane):
        sib_copy(o).wait_send()
        if o > 0:
            col_copy((0, 0), offsets[o]).wait_send()
        for b in range(2):
            if (b, o) != (0, 0):
                col_part_copy(b, o).wait_send()


def per_device(points, solution, residual, direction):
    vmem = pl.BlockSpec(memory_space=pltpu.VMEM)
    dma = pltpu.SemaphoreType.DMA
    out = jax.ShapeDtypeStruct((rhs, block), f32)
    span = rows_n * block
    applied, step_size, ratio = pl.pallas_call(
        kernel,
        out_shape=(out, out, out),
        in_specs=[pl.BlockSpec(memory_space=pltpu.HBM)] * 3,
        out_specs=(vmem, vmem, vmem),
        scratch_shapes=[
            pltpu.VMEM((2, plane, block + rhs, block), f32),
            pltpu.VMEM((held, block + rhs, block), f32),
            pltpu.VMEM((pairs, 4 * block, 2 * block), bf16),
            pltpu.VMEM((pairs, 8, 2 * block), f32),
            pltpu.VMEM((pairs, 2 * rhs, 2 * block), bf16),
            pltpu.VMEM((span, 4 * block), bf16),
            pltpu.VMEM((span, block), f32),
            pltpu.VMEM((2 * rhs, span), bf16),
            pltpu.VMEM((4 * block, block), bf16),
            pltpu.VMEM((8, block), f32),
            pltpu.VMEM((chunk, 2 * block), f32),
            pltpu.VMEM((chunk, 2 * block), f32),
            pltpu.VMEM((chunk, block), f32),
            pltpu.VMEM((chunk, block), f32),
            pltpu.VMEM((2, chunks, chunk, 2 * block), bf16),
            pltpu.VMEM((pairs, 2 * rhs, 2 * block), f32),
            pltpu.VMEM((2 * rhs, span), f32),
            pltpu.VMEM((2 * rhs, block), f32),
            pltpu.VMEM((held, rhs, block), f32),
            pltpu.VMEM((held, rhs, block), f32),
            pltpu.VMEM((2, plane, rhs, block), f32),
            pltpu.VMEM((2, plane, rhs, block), f32),
            pltpu.VMEM((cols_n, 1, block), f32),
            pltpu.VMEM((rows_n, 1, block), f32),
            pltpu.VMEM((rhs, block), f32),
            dma((3,)),
            dma((plane,)),
            dma((plane,)),
            dma((plane,)),
            dma((plane,)),
            dma((held, 2)),
            dma((held, 2)),
            dma((held,)),
            dma((held,)),
            dma((2, plane)),
            dma((2, plane)),
            dma((cols_n,)),
            dma((cols_n,)),
            dma((rows_n,)),
            dma((rows_n,)),
        ],
        compiler_params=pltpu.CompilerParams(
            collective_id=0, has_side_effects=True, vmem_limit_bytes=60 * 1024 * 1024
        ),
        name="cg_step",
    )(points, residual, direction)
    next_residual = residual - step_size * applied
    return solution + step_size * direction, next_residual, next_residual + ratio * direction


def solution(mesh):
    spec = P(None, ("row", "col"))
    return jax.shard_map(
        per_device, mesh=mesh, in_specs=(spec,) * 4, out_specs=(spec,) * 3, check_vma=False
    )
```

```python
import math

import jax
import jax.numpy as jnp
from jax import lax
from jax.experimental import pallas as pl
from jax.experimental.pallas import tpu as pltpu
from jax.sharding import PartitionSpec as P

noise_var = 0.5
inv_two_len = 0.03125
scale = inv_two_len * math.log2(math.e)

MESH = pl.DeviceIdType.MESH
f32 = jnp.float32
bf16 = jnp.bfloat16

side = 4
rows_n = 32
cols_n = 16
block = 128
rhs = 16
chunk = 1024
chunks = 4
pairs = 4
held = 9
half_rows = (block + rhs) // 2

offsets = [
    (0, 0), (1, 0), (3, 0), (0, 1),
    (0, 3), (1, 1), (3, 3), (1, 3),
    (3, 1), (2, 0), (0, 2), (2, 1),
    (2, 3), (3, 2), (1, 2), (2, 2),
]
plane = len(offsets)
near = [(1, 0), (3, 0), (0, 1), (0, 3)]
diagonal = [(1, 1), (3, 3), (3, 1), (1, 3)]
far = [o for o in offsets if o not in near + diagonal + [(0, 0)]]
relays = {
    (3, 0): [(3, 0)],
    (0, 3): [(0, 3)],
    (1, 1): [(1, 0), (1, 1)],
    (3, 3): [(3, 0)],
    (3, 1): [(0, 1)],
    (1, 3): [(0, 3)],
}

def slot_of(offset):
    return offsets.index((offset[0] % side, offset[1] % side))


def split(values):
    high = values.astype(bf16)
    low = (values - high.astype(f32)).astype(bf16)
    return high, low


def dot(a, b):
    return jnp.dot(a, b, preferred_element_type=f32)


def dot_turned(a, b):
    return lax.dot_general(a, b, (((1,), (1,)), ((), ())), preferred_element_type=f32)


def kernel(
    pts_hbm,
    res_hbm,
    dir_hbm,
    applied_ref,
    step_ref,
    ratio_ref,
    col_in,
    row_in,
    weights,
    row_sq,
    row_dirs,
    stream,
    col_sq,
    dirs,
    own_weights,
    own_sq,
    tile_a,
    tile_b,
    own_a,
    own_b,
    kept,
    row_total,
    col_total,
    own_total,
    part,
    part_in,
    col_part,
    col_part_in,
    stat_z,
    stat_r,
    res_ref,
    load,
    col_send,
    col_recv,
    sib_send,
    sib_recv,
    row_send,
    row_recv,
    part_send,
    part_recv,
    cp_send,
    cp_recv,
    sz_send,
    sz_recv,
    sr_send,
    sr_recv,
):
    r = lax.axis_index("row")
    z = lax.axis_index("col")
    x, y, core = r // 8, (r // 2) % 4, r % 2
    sibling = r + 1 - 2 * core

    def device_at(offset, other):
        target = (((x + offset[0]) % side) * side + (y + offset[1]) % side) * 2
        return target + (1 - core if other else core)

    loads = [
        pltpu.make_async_copy(src, dst, load.at[i])
        for i, (src, dst) in enumerate(
            (
                (pts_hbm, row_in.at[0, 0:block]),
                (dir_hbm, row_in.at[0, block : block + rhs]),
                (res_hbm, res_ref),
            )
        )
    ]
    for copy in loads:
        copy.start()

    barrier = pltpu.get_barrier_semaphore()
    for step in (2, 14, 1, 15):
        pl.semaphore_signal(barrier, inc=1, device_id=(r, (z + step) % cols_n), device_id_type=MESH)
    for offset in diagonal + near:
        pl.semaphore_signal(barrier, inc=1, device_id=(device_at(offset, False), z), device_id_type=MESH)
    pl.semaphore_signal(barrier, inc=1, device_id=(sibling, z), device_id_type=MESH)

    for copy in loads:
        copy.wait()
    col_in[0, 0, 0:block, :] = row_in[0, 0:block, :].T
    col_in[0, 0, block : block + rhs, :] = row_in[0, block : block + rhs, :]
    row_total[...] = jnp.zeros_like(row_total)
    col_total[...] = jnp.zeros_like(col_total)
    own_total[...] = jnp.zeros_like(own_total)

    pl.semaphore_wait(barrier, 13)

    def row_copy(src, dst, half, step):
        place = pl.ds(half * half_rows, half_rows)
        return pltpu.make_async_remote_copy(
            src_ref=row_in.at[src, place],
            dst_ref=row_in.at[dst, place],
            send_sem=row_send.at[dst, half],
            recv_sem=row_recv.at[dst, half],
            device_id=(r, (z + cols_n + step) % cols_n),
            device_id_type=MESH,
        )

    def col_copy(offset, step):
        dst = slot_of((offset[0] + step[0], offset[1] + step[1]))
        return pltpu.make_async_remote_copy(
            src_ref=col_in.at[0, slot_of(offset)],
            dst_ref=col_in.at[0, dst],
            send_sem=col_send.at[dst],
            recv_sem=col_recv.at[dst],
            device_id=(device_at((side - step[0], side - step[1]), False), z),
            device_id_type=MESH,
        )

    def sib_copy(o):
        return pltpu.make_async_remote_copy(
            src_ref=col_in.at[0, o],
            dst_ref=col_in.at[1, o],
            send_sem=sib_send.at[o],
            recv_sem=sib_recv.at[o],
            device_id=(sibling, z),
            device_id_type=MESH,
        )

    def part_copy(k):
        return pltpu.make_async_remote_copy(
            src_ref=part.at[k],
            dst_ref=part_in.at[k],
            send_sem=part_send.at[k],
            recv_sem=part_recv.at[k],
            device_id=(r, (z + (cols_n - k if k % 2 else k)) % cols_n),
            device_id_type=MESH,
        )

    def col_part_copy(b, o):
        dx, dy = offsets[o]
        dst = slot_of((-dx, -dy))
        return pltpu.make_async_remote_copy(
            src_ref=col_part.at[b, o],
            dst_ref=col_part_in.at[b, dst],
            send_sem=cp_send.at[b, o],
            recv_sem=cp_recv.at[b, dst],
            device_id=(device_at((dx, dy), b == 1), z),
            device_id_type=MESH,
        )

    for half in range(2):
        row_copy(0, 1, half, 1).start()
        row_copy(0, 2, half, -2).start()
    sib_copy(0).start()
    for offset in near + diagonal:
        col_copy((0, 0), offset).start()

    def turn(pts):
        high, low = split(pts * (2.0 * scale))
        stacked = jnp.concatenate([high, low, high, low], axis=0)
        return stacked, jnp.broadcast_to(scale * jnp.sum(pts * pts, axis=0, keepdims=True), (8, block))

    def make_weights(p):
        for half in range(2):
            k = 2 * p + 1 + half
            lanes = slice(half * block, (half + 1) * block)
            weights[p, :, lanes], row_sq[p, :, lanes] = turn(row_in[k, 0:block, :])
            if k < 8:
                high, low = split(row_in[k, block : block + rhs, :])
            else:
                high = low = jnp.zeros((rhs, block), bf16)
            row_dirs[p, 0:rhs, lanes] = high
            row_dirs[p, rhs : 2 * rhs, lanes] = low

    def make_stream(b, o):
        place = pl.ds(pl.multiple_of((2 * o + b) * block, block), block)
        pts = col_in[b, o, 0:block, :]
        high, low = split(pts)
        stream[place, 0 * block : 1 * block] = high
        stream[place, 1 * block : 2 * block] = high
        stream[place, 2 * block : 3 * block] = low
        stream[place, 3 * block : 4 * block] = low
        col_sq[place, :] = jnp.broadcast_to(scale * jnp.sum(pts * pts, axis=1, keepdims=True), (block, block))
        high, low = split(col_in[b, o, block : block + rhs, :])
        dirs[0:rhs, place] = high
        dirs[rhs : 2 * rhs, place] = low

    def take_columns(arrived):
        for offset in arrived:
            col_copy((0, 0), offset).wait_recv()
            for step in relays.get(offset, ()):
                col_copy(offset, step).start()
            sib_copy(slot_of(offset)).start()

    def use_columns(c):
        for o in range(4 * c, 4 * c + 4):
            make_stream(0, o)
        for o in range(4 * c, 4 * c + 4):
            sib_copy(o).wait_recv()
        for o in range(4 * c, 4 * c + 4):
            make_stream(1, o)

    def take_row(k, half):
        row_copy(0, k, half, 0).wait_recv()
        if k + 2 < held:
            row_copy(k, k + 2, half, 2 if k % 2 else -2).start()

    def send_rows(p):
        both = row_total[p]
        both = both[0:rhs] + both[rhs : 2 * rhs]
        for half in range(2):
            k = 2 * p + 1 + half
            part[k] = both[:, half * block : (half + 1) * block]
        for half in range(2):
            part_copy(2 * p + 1 + half).start()

    def send_columns(c):
        for o in range(4 * c, 4 * c + 4):
            for b in range(2):
                place = slice((2 * o + b) * block, (2 * o + b + 1) * block)
                col_part[b, o] = col_total[0:rhs, place] + col_total[rhs : 2 * rhs, place]
        for o in range(4 * c + 3, 4 * c - 1, -1):
            for b in range(2):
                if (b, o) != (0, 0):
                    col_part_copy(b, o).start()

    def products(p, c, tile):
        place = pl.ds(c * chunk, chunk)
        tile[...] = dot(stream[place, :], weights[p])

    def apply(p, c, tile):
        place = pl.ds(c * chunk, chunk)
        sq = col_sq[place, :]
        exponent = tile[...] - jnp.concatenate([sq, sq], axis=1) - row_sq[p, 0:1, :]
        high, low = split(jnp.exp2(exponent))
        row_total[p] += dot(dirs[:, place], high) + dot(dirs[:, place], low)
        col_total[:, place] += dot_turned(row_dirs[p], high) + dot_turned(row_dirs[p], low)

    def late_apply(c, tile):
        place = pl.ds(c * chunk, chunk)
        sq = col_sq[place, :]
        exponent = tile[...] - jnp.concatenate([sq, sq], axis=1) - row_sq[3, 0:1, :]
        high, low = split(jnp.exp2(exponent))
        kept[0, c], kept[1, c] = high, low
        row_total[3] += dot(dirs[:, place], high) + dot(dirs[:, place], low)

    def late_columns(c):
        place = pl.ds(c * chunk, chunk)
        col_total[:, place] += dot_turned(row_dirs[3], kept[0, c]) + dot_turned(row_dirs[3], kept[1, c])

    own_weights[...], own_sq[...] = turn(row_in[0, 0:block, :])

    def own_products(c, tile):
        place = pl.ds(c * chunk, chunk)
        tile[...] = dot(stream[place, :], own_weights[...])

    def own_apply(c, tile):
        place = pl.ds(c * chunk, chunk)
        high, low = split(jnp.exp2(tile[...] - col_sq[place, :] - own_sq[0:1, :]))
        own_total[...] += dot(dirs[:, place], high) + dot(dirs[:, place], low)

    waiting = []

    def flush():
        while waiting:
            waiting.pop()()

    def unit(p, c, tile):
        products(p, c, tile)
        flush()
        waiting.append(lambda: apply(p, c, tile))

    def late_unit(c, tile):
        products(3, c, tile)
        flush()
        waiting.append(lambda: late_apply(c, tile))

    def own(c, tile):
        own_products(c, tile)
        flush()
        waiting.append(lambda: own_apply(c, tile))

    take_row(1, 0)
    take_row(1, 1)
    take_row(2, 0)
    take_columns(near)
    take_row(2, 1)
    make_weights(0)
    use_columns(0)
    unit(0, 0, tile_a)
    own(0, own_a)
    flush()
    take_row(3, 0)
    take_columns(diagonal)
    take_row(4, 0)
    take_row(3, 1)
    use_columns(1)
    unit(0, 1, tile_b)
    flush()
    take_row(4, 1)
    take_columns(far[:2])
    make_weights(1)
    unit(1, 0, tile_a)
    own(1, own_b)
    flush()
    take_row(5, 0)
    take_columns(far[2:3])
    use_columns(2)
    unit(0, 2, tile_b)
    take_row(6, 0)
    take_row(5, 1)
    take_columns(far[3:])
    unit(1, 2, tile_a)
    take_row(6, 1)
    make_weights(2)
    use_columns(3)
    unit(2, 2, tile_b)
    unit(2, 0, tile_a)
    unit(2, 3, tile_b)
    unit(2, 1, tile_a)
    unit(0, 3, tile_b)
    send_rows(2)
    flush()
    send_rows(0)
    for half in range(2):
        take_row(7, half)
        take_row(8, half)
    make_weights(3)
    for c, tile in ((0, tile_a), (1, tile_b), (2, tile_a), (3, tile_b)):
        late_unit(c, tile)
    flush()
    send_rows(3)
    unit(1, 3, tile_a)
    unit(1, 1, tile_b)
    late_columns(3)
    send_columns(3)
    late_columns(2)
    send_columns(2)
    own(2, own_a)
    send_rows(1)
    late_columns(1)
    send_columns(1)
    late_columns(0)
    send_columns(0)
    own(3, own_b)
    flush()

    direction = row_in[0, block : block + rhs, :]
    residual = res_ref[...]
    applied = own_total[0:rhs] + own_total[rhs : 2 * rhs] + col_part[0, 0] + noise_var * direction
    for o in range(plane):
        for b in range(2):
            if (b, o) != (0, 0):
                col_part_copy(b, o).wait_recv()
    for b in range(2):
        for o in range(plane):
            if (b, o) != (0, 0):
                applied = applied + col_part_in[b, o]
    for k in range(1, held):
        part_copy(k).wait_recv()
    for k in range(1, held):
        applied = applied + part_in[k]

    lane = lax.broadcasted_iota(jnp.int32, (rhs, block), 1)
    line = lax.broadcasted_iota(jnp.int32, (rhs, block), 0)
    packed = jnp.zeros((rhs, block), f32)
    for q, values in enumerate((residual * residual, direction * applied, residual * applied, applied * applied)):
        packed = jnp.where(lane == line + q * rhs, jnp.sum(values, axis=1, keepdims=True), packed)
    stat_z[0] = jnp.sum(packed, axis=0, keepdims=True)

    def z_copy(step):
        return pltpu.make_async_remote_copy(
            src_ref=stat_z.at[0],
            dst_ref=stat_z.at[step],
            send_sem=sz_send.at[step],
            recv_sem=sz_recv.at[step],
            device_id=(r, (z + step) % cols_n),
            device_id_type=MESH,
        )

    def r_copy(b, o):
        dx, dy = offsets[o]
        dst = 2 * slot_of((-dx, -dy)) + b
        return pltpu.make_async_remote_copy(
            src_ref=stat_r.at[0],
            dst_ref=stat_r.at[dst],
            send_sem=sr_send.at[2 * o + b],
            recv_sem=sr_recv.at[dst],
            device_id=(device_at((dx, dy), b == 1), z),
            device_id_type=MESH,
        )

    others = [(b, o) for o in range(plane - 1, -1, -1) for b in range(2) if (b, o) != (0, 0)]
    for step in sorted(range(1, cols_n), key=lambda step: -min(step, cols_n - step)):
        z_copy(step).start()
    for k in range(1, held):
        for half in range(2):
            row_copy(0, k, half, 0).wait_send()
        part_copy(k).wait_send()
    for o in range(plane):
        sib_copy(o).wait_send()
        if o > 0:
            col_copy((0, 0), offsets[o]).wait_send()
        for b in range(2):
            if (b, o) != (0, 0):
                col_part_copy(b, o).wait_send()
    for step in range(1, cols_n):
        z_copy(step).wait_recv()
    stat_r[0] = jnp.sum(stat_z[...], axis=0)
    for b, o in others:
        r_copy(b, o).start()
    for step in range(1, cols_n):
        z_copy(step).wait_send()
    for b, o in others:
        r_copy(b, o).wait_send()
    for b, o in others:
        r_copy(b, o).wait_recv()
    sums = jnp.broadcast_to(jnp.sum(stat_r[...], axis=0), (rhs, block))

    def take(q):
        return jnp.sum(jnp.where(lane == line + q * rhs, sums, 0.0), axis=1, keepdims=True)

    norm_now, curvature, cross, square = take(0), take(1), take(2), take(3)
    step_size = norm_now / curvature
    norm_next = jnp.maximum(norm_now - step_size * (2.0 * cross - step_size * square), 0.0)
    ratio = norm_next / norm_now
    applied_ref[...] = applied
    step_ref[...] = jnp.broadcast_to(step_size, (rhs, block))
    ratio_ref[...] = jnp.broadcast_to(ratio, (rhs, block))


def per_device(points, solution, residual, direction):
    vmem = pl.BlockSpec(memory_space=pltpu.VMEM)
    dma = pltpu.SemaphoreType.DMA
    out = jax.ShapeDtypeStruct((rhs, block), f32)
    span = rows_n * block
    applied, step_size, ratio = pl.pallas_call(
        kernel,
        out_shape=(out, out, out),
        in_specs=[pl.BlockSpec(memory_space=pltpu.HBM)] * 3,
        out_specs=(vmem, vmem, vmem),
        scratch_shapes=[
            pltpu.VMEM((2, plane, block + rhs, block), f32),
            pltpu.VMEM((held, block + rhs, block), f32),
            pltpu.VMEM((pairs, 4 * block, 2 * block), bf16),
            pltpu.VMEM((pairs, 8, 2 * block), f32),
            pltpu.VMEM((pairs, 2 * rhs, 2 * block), bf16),
            pltpu.VMEM((span, 4 * block), bf16),
            pltpu.VMEM((span, block), f32),
            pltpu.VMEM((2 * rhs, span), bf16),
            pltpu.VMEM((4 * block, block), bf16),
            pltpu.VMEM((8, block), f32),
            pltpu.VMEM((chunk, 2 * block), f32),
            pltpu.VMEM((chunk, 2 * block), f32),
            pltpu.VMEM((chunk, block), f32),
            pltpu.VMEM((chunk, block), f32),
            pltpu.VMEM((2, chunks, chunk, 2 * block), bf16),
            pltpu.VMEM((pairs, 2 * rhs, 2 * block), f32),
            pltpu.VMEM((2 * rhs, span), f32),
            pltpu.VMEM((2 * rhs, block), f32),
            pltpu.VMEM((held, rhs, block), f32),
            pltpu.VMEM((held, rhs, block), f32),
            pltpu.VMEM((2, plane, rhs, block), f32),
            pltpu.VMEM((2, plane, rhs, block), f32),
            pltpu.VMEM((cols_n, 1, block), f32),
            pltpu.VMEM((rows_n, 1, block), f32),
            pltpu.VMEM((rhs, block), f32),
            dma((3,)),
            dma((plane,)),
            dma((plane,)),
            dma((plane,)),
            dma((plane,)),
            dma((held, 2)),
            dma((held, 2)),
            dma((held,)),
            dma((held,)),
            dma((2, plane)),
            dma((2, plane)),
            dma((cols_n,)),
            dma((cols_n,)),
            dma((rows_n,)),
            dma((rows_n,)),
        ],
        compiler_params=pltpu.CompilerParams(
            collective_id=0, has_side_effects=True, vmem_limit_bytes=60 * 1024 * 1024
        ),
        name="cg_step",
    )(points, residual, direction)
    next_residual = residual - step_size * applied
    return solution + step_size * direction, next_residual, next_residual + ratio * direction


def solution(mesh):
    spec = P(None, ("row", "col"))
    return jax.shard_map(
        per_device, mesh=mesh, in_specs=(spec,) * 4, out_specs=(spec,) * 3, check_vma=False
    )
```
